128 devices in a mesh: az: 8 (over z, core), rg: 16 (over y, x).
Axes of the slice: x: 4, y: 4, z: 4, core: 2. Of those that a mesh axis runs over, the one named last changes fastest.
Arguments:
- raw: bfloat16 [2, 16384, 8320], P(None, ('az', 'rg')), may hold values from -6 to 6
- range_filter: bfloat16 [2, 4096], replicated, may hold values from -0.0625 to 0.0625
- mig_offsets: int32 [32], replicated, may hold values from 0 to 96
- mig_widths: int32 [32], replicated, may hold values from 1 to 32
- mig_coefs: bfloat16 [32, 32], replicated, may hold values from -1.5 to 1.5
- az_filter: bfloat16 [2, 4096, 4096], P(None, None, 'rg'), may hold values from -0.09375 to 0.09375
- az_lengths: int32 [4096], P('rg'), may hold values from 1024 to 4096
Outputs:
- image: float32 [2, 16384, 4096], P(None, 'az', 'rg')
The draws below stay inside these ranges and needn't reach their ends.
All inputs are finite; a program needn't handle non-finite values.
Results may differ from the reference program's by a relative error of at most 0.0041.
Values may be sent and summed in bfloat16 or wider, within the bound.
No kernel may reach another device: no remote copies, remote signals or barrier semaphores. Data moves between devices by JAX's collectives and lax.ppermute only.
A program may use at most 192 MiB of HBM per device.

```python
import jax
import jax.numpy as jnp
from jax import lax

CHIRP = 4096
LMAX = 4096
MIGBLK = 128
OFFMAX = 96
WMAX = 32
RBD = 256
PTOT = 16384
RW = 4096
NBLK = 32
RIN = 8320
N_AZ = 8
N_RG = 16


def draw_mig_offsets(key, part):
    key = jax.random.fold_in(key, 11)
    first, second = jax.random.split(key)
    count = RW // MIGBLK
    values = jax.random.randint(first, (count,), 0, OFFMAX + 1)
    where_top = jax.random.randint(second, (), 0, count)
    return jnp.where(jnp.arange(count) == where_top, OFFMAX, values).astype(jnp.int32)


def draw_mig_widths(key, part):
    key = jax.random.fold_in(key, 23)
    first, second = jax.random.split(key)
    count = RW // MIGBLK
    values = jax.random.randint(first, (count,), 1, WMAX + 1)
    where_top = jax.random.randint(second, (), 0, count)
    return jnp.where(jnp.arange(count) == where_top, WMAX, values).astype(jnp.int32)


def draw_az_lengths(key, part):
    key = jax.random.fold_in(key, 37)
    first, second, third = jax.random.split(key, 3)
    position = jnp.arange(RW)
    base = LMAX // 4 + 3 * LMAX // 4 * position // RW
    jitter = jax.random.randint(first, (RW,), -(LMAX // 8), LMAX // 8 + 1)
    values = jnp.clip(base + jitter, LMAX // 4, LMAX)
    longest = jax.random.randint(second, (), RW - RBD, RW)
    shortest = jax.random.randint(third, (), 0, RBD)
    values = jnp.where(position == longest, LMAX, values)
    values = jnp.where(position == shortest, LMAX // 4, values)
    return values.astype(jnp.int32)


def level_of(key, extent, shards, smallest, largest):
    def one(axis_at, parts):
        steps = jax.random.uniform(jax.random.fold_in(jax.random.fold_in(key, 6), axis_at), (parts,), jnp.float32, smallest / len(shards), largest / len(shards))
        return jnp.repeat(jnp.exp(steps), extent[axis_at] // parts).reshape((-1,) + (1,) * (len(extent) - axis_at - 1))

    gain = one(*shards[0])
    for cut in shards[1:]:
        gain = gain * one(*cut)
    return gain


def scatter_about(stream_key, dims, scale, bound, cuts=(), kind=jnp.bfloat16):
    level = level_of(stream_key, dims, cuts, -0.22, 0.18) if cuts else 1.0
    drawn = jax.random.normal(stream_key, dims, jnp.float32) * scale * level
    return jnp.minimum(jnp.maximum(drawn, -bound), bound).astype(kind)


def setup_inputs(seed: int = 0) -> dict:
    splits = jax.random.split(jax.random.key(seed), 8)
    raw = scatter_about(splits[0], (2, PTOT, RIN), 1.0, 6.0, ((1, 128),))
    range_filter = scatter_about(splits[1], (2, CHIRP), (2 * CHIRP) ** -0.5, 0.0625)
    mig_offsets = draw_mig_offsets(jax.random.fold_in(splits[7], 71), 0)
    mig_widths = draw_mig_widths(jax.random.fold_in(splits[7], 71), 0)
    mig_coefs = scatter_about(splits[4], (NBLK, WMAX), (WMAX // 2) ** -0.5, 1.5)
    az_filter = scatter_about(splits[5], (2, LMAX, RW), LMAX ** -0.5, 0.09375, ((2, 16),))
    az_lengths = draw_az_lengths(jax.random.fold_in(splits[7], 71), 0)
    return {"raw": raw, "range_filter": range_filter, "mig_offsets": mig_offsets, "mig_widths": mig_widths, "mig_coefs": mig_coefs, "az_filter": az_filter, "az_lengths": az_lengths}


def band_matrices(offsets, widths, coefs):
    count = offsets.shape[0]
    lag = (jnp.arange(2 * MIGBLK)[None, :, None] - jnp.arange(MIGBLK)[None, None, :]
           - offsets[:, None, None])
    matrix = jnp.zeros((count, 2 * MIGBLK, MIGBLK), jnp.float32)
    for band in range(coefs.shape[1]):
        chosen = (lag == band) & (band < widths[:, None, None])
        matrix = matrix + jnp.where(chosen, coefs[:, band].astype(jnp.float32)[:, None, None], 0.0)
    return matrix


def migrate(compressed, offsets, widths, coefs):
    count = offsets.shape[0]
    rows = compressed.shape[1]
    lower = compressed[:, :, :count * MIGBLK].reshape(2, rows, count, MIGBLK)
    upper = compressed[:, :, MIGBLK:(count + 1) * MIGBLK].reshape(2, rows, count, MIGBLK)
    windows = jnp.concatenate([lower, upper], axis=3).astype(jnp.float32)
    matrix = band_matrices(offsets, widths, coefs)
    moved = jnp.einsum('crbi,biq->crbq', windows, matrix, precision=lax.Precision.HIGHEST)
    return moved.reshape(2, rows, count * MIGBLK).astype(jnp.bfloat16)


def reference(raw, range_filter, mig_offsets, mig_widths, mig_coefs, az_filter, az_lengths):
    samples = raw.shape[2]
    keep = RW + MIGBLK
    pulses = LMAX // 2
    filt_complex = lax.complex(range_filter[0].astype(jnp.float32), range_filter[1].astype(jnp.float32))
    padded = jnp.zeros((samples,), filt_complex.dtype).at[:CHIRP].set(filt_complex)
    response = samples * jnp.fft.ifft(padded)
    blocks = raw.reshape(2, N_AZ, pulses, samples).transpose(1, 0, 2, 3)

    def compress_block(block):
        signal = lax.complex(block[0].astype(jnp.float32), block[1].astype(jnp.float32))
        result = jnp.fft.ifft(jnp.fft.fft(signal, axis=-1) * response[None, :], axis=-1)[:, :keep]
        return jnp.stack([jnp.real(result), jnp.imag(result)]).astype(jnp.bfloat16)

    compressed = lax.map(compress_block, blocks)

    def migrate_block(block):
        return migrate(block, mig_offsets, mig_widths, mig_coefs)

    migrated = lax.map(migrate_block, compressed)
    migrated = migrated.transpose(1, 0, 2, 3).reshape(2, PTOT, RW)

    length_mask = jnp.arange(LMAX)[:, None] < az_lengths[None, :]
    taps = jnp.where(length_mask[None], az_filter.astype(jnp.float32), 0.0)
    total = PTOT + LMAX
    signal_blocks = migrated.reshape(2, PTOT, N_RG, RBD).transpose(2, 0, 1, 3)
    tap_blocks = taps.reshape(2, LMAX, N_RG, RBD).transpose(2, 0, 1, 3)

    def focus_block(pair):
        block, tap_block = pair
        signal = lax.complex(block[0].astype(jnp.float32), block[1].astype(jnp.float32))
        signal = jnp.pad(signal, ((0, LMAX), (0, 0)))
        kernel = lax.complex(tap_block[0], tap_block[1])
        kernel = jnp.pad(kernel, ((0, PTOT), (0, 0)))
        kernel_spectrum = total * jnp.fft.ifft(kernel, axis=0)
        result = jnp.fft.ifft(jnp.fft.fft(signal, axis=0) * kernel_spectrum, axis=0)[:PTOT]
        return jnp.stack([jnp.real(result), jnp.imag(result)]).astype(jnp.float32)

    focused = lax.map(focus_block, (signal_blocks, tap_blocks))
    return focused.transpose(1, 2, 0, 3).reshape(2, PTOT, RW)
```

```python
import functools
import math

import jax
import jax.numpy as jnp
import numpy as np
from jax import lax
from jax.experimental import pallas as pl
from jax.experimental.pallas import tpu as pltpu
from jax.sharding import PartitionSpec as P

BF = jnp.bfloat16
F32 = jnp.float32
BLK = 128
TAPB = 32
NBLK = 32
NOUT = 33
NSAMP = 65
N1 = 160
MSRC = 128
MOUT = 128
MFIL = 32
NBIN = 32
VMEM = 50 * 1024 * 1024
NT = (((1,), (1,)), ((), ()))


def dot(a, b):
    return jnp.dot(a, b, preferred_element_type=F32)


def filter_rows(range_filter):
    padded = jnp.pad(range_filter.astype(F32), ((0, 0), (BLK - 1, BLK + 1)))
    first = padded[:, : NOUT * BLK].reshape(2, NOUT, BLK)[:, :, ::-1]
    second = padded[:, BLK:].reshape(2, NOUT, BLK)[:, :, ::-1]
    return jnp.concatenate([first, second], axis=2).transpose(1, 0, 2)


def compress_kernel(off_ref, wid_ref, base_ref, coef_ref, raw_ref, out_ref, x_ref, g_ref, c_ref):
    def arrange(s, _):
        o = pl.multiple_of(s * BLK, BLK)
        x_ref[pl.ds(o, BLK), 0:BLK] = raw_ref[0, :, pl.ds(o, BLK)]
        x_ref[pl.ds(o, BLK), BLK:] = raw_ref[1, :, pl.ds(o, BLK)]
        return 0

    lax.fori_loop(0, NSAMP, arrange, 0, unroll=5)

    def table(j, _):
        o = pl.multiple_of(j * 2 * BLK, 2 * BLK)
        rows = base_ref[j]

        def spread(row):
            wide = jnp.broadcast_to(row, (BLK, 2 * BLK))
            return pltpu.roll(wide, 0, 1, stride=1, stride_axis=0)[:, :BLK]

        re = spread(rows[0:1])
        im = spread(rows[1:2])
        g_ref[pl.ds(o, BLK), 0:BLK] = re.astype(BF)
        g_ref[pl.ds(o, BLK), BLK:] = im.astype(BF)
        g_ref[pl.ds(o + BLK, BLK), 0:BLK] = (-im).astype(BF)
        g_ref[pl.ds(o + BLK, BLK), BLK:] = re.astype(BF)
        return 0

    lax.fori_loop(0, NOUT, table, 0, unroll=3)

    group = 11
    rows = group * BLK

    def multiply(g, _):
        r0 = pl.multiple_of(g * rows, BLK)
        acc = jnp.zeros((rows, 2 * BLK), F32)
        for j in range(NOUT):
            acc = acc + dot(x_ref[pl.ds(r0 + j * BLK, rows), :], g_ref[j * 2 * BLK : (j + 1) * 2 * BLK, :])
        out = acc.astype(BF)
        for b in range(group):
            part = out[b * BLK : (b + 1) * BLK]
            c_ref[g * group + b, 0:BLK, :] = part[:, :BLK]
            c_ref[g * group + b, BLK:, :] = part[:, BLK:]
        return 0

    lax.fori_loop(0, NOUT // group, multiply, 0)

    lane = lax.broadcasted_iota(jnp.int32, (1, 2 * BLK), 1)

    def migrate(b, _):
        row = jnp.where(lane < wid_ref[b], coef_ref[pl.ds(b, 1), :], 0.0)
        row = pltpu.roll(jnp.broadcast_to(row, (8, 2 * BLK)), off_ref[b], 1)[0:1]
        wide = jnp.broadcast_to(row, (BLK, 2 * BLK))
        band = pltpu.roll(wide, 0, 1, stride=1, stride_axis=0).astype(BF)
        window = jnp.concatenate([c_ref[b], c_ref[b + 1]], axis=1)
        moved = lax.dot_general(band, window, NT, preferred_element_type=F32)
        out_ref[pl.ds(pl.multiple_of(b * BLK, BLK), BLK), :] = moved.astype(BF)
        return 0

    lax.fori_loop(0, NBLK, migrate, 0, unroll=4)


def compress(raw, range_filter, offsets, widths, coefs):
    wide_coefs = jnp.pad(coefs.astype(F32), ((0, 0), (0, 2 * BLK - coefs.shape[1])))
    vmem = pl.BlockSpec(memory_space=pltpu.VMEM)
    smem = pl.BlockSpec(memory_space=pltpu.SMEM)
    return pl.pallas_call(
        compress_kernel,
        out_shape=jax.ShapeDtypeStruct((NBLK * BLK, 2 * BLK), BF),
        in_specs=[smem, smem, vmem, vmem, vmem],
        out_specs=vmem,
        scratch_shapes=[
            pltpu.VMEM((NSAMP * BLK, 2 * BLK), BF),
            pltpu.VMEM((NOUT * 2 * BLK, 2 * BLK), BF),
            pltpu.VMEM((NOUT, 2 * BLK, BLK), BF),
        ],
        compiler_params=pltpu.CompilerParams(vmem_limit_bytes=VMEM),
        cost_estimate=pl.CostEstimate(flops=18_300_000_000, bytes_accessed=8_000_000, transcendentals=0),
    )(offsets, widths, filter_rows(range_filter), wide_coefs, raw)


def split(table):
    hi = table.astype(np.float32).astype(jnp.bfloat16)
    lo = (table - hi.astype(np.float64)).astype(np.float32).astype(jnp.bfloat16)
    return hi, lo


def angles(rows, cols, period):
    return 2.0 * np.pi * (np.outer(rows, cols) % period) / period


def left_table(theta, sign):
    c, s = np.cos(theta), sign * np.sin(theta)
    return np.concatenate(split(np.block([[c, -s], [s, c]])), axis=0)


def right_table(theta, sign):
    c, s = np.cos(theta), sign * np.sin(theta)
    return np.concatenate(split(np.block([[c, s], [-s, c]])), axis=1)


def source_order(n_az, n_rg):
    s = np.arange(n_az * n_rg)
    return (s % n_az) * n_rg + s // n_az


def twiddle():
    theta = angles(np.arange(N1), np.arange(BLK), N1 * BLK)
    return np.stack([np.cos(theta), np.sin(theta)]).astype(np.float32)


def filter_kernel(taps_ref, w1_ref, tw_ref, wp_ref, h_ref):
    def pair(i, _):
        both = jnp.concatenate([taps_ref[2 * i], taps_ref[2 * i + 1]], axis=1)
        first = dot(w1_ref[...], both)
        first = first[: 2 * N1] + first[2 * N1 :]
        for u in range(2):
            re = first[:N1, u * BLK : (u + 1) * BLK]
            im = first[N1:, u * BLK : (u + 1) * BLK]
            c, s = tw_ref[0], tw_ref[1]
            turned = jnp.concatenate([re * c - im * s, im * c + re * s], axis=1)
            hi = turned.astype(BF)
            lo = (turned - hi.astype(F32)).astype(BF)
            second = dot(hi, wp_ref[...])
            third = dot(lo, wp_ref[:, : 2 * BLK])
            h_ref[2 * i + u] = (second[:, : 2 * BLK] + second[:, 2 * BLK :] + third) * (1.0 / (N1 * BLK))
        return 0

    lax.fori_loop(0, NBIN // 2, pair, 0)


def filter_spectrum(taps):
    w1 = left_table(angles(np.arange(N1), np.arange(MFIL), N1), 1.0)
    wp = right_table(angles(np.arange(BLK), np.arange(BLK), BLK), 1.0)
    vmem = pl.BlockSpec(memory_space=pltpu.VMEM)
    return pl.pallas_call(
        filter_kernel,
        out_shape=jax.ShapeDtypeStruct((NBIN, N1, 2 * BLK), F32),
        in_specs=[vmem] * 4,
        out_specs=vmem,
        compiler_params=pltpu.CompilerParams(vmem_limit_bytes=VMEM),
        cost_estimate=pl.CostEstimate(flops=4_000_000_000, bytes_accessed=8_000_000, transcendentals=0),
    )(taps, jnp.asarray(w1), jnp.asarray(twiddle()), jnp.asarray(wp))


def focus_kernel(x_ref, h_ref, w1_ref, tw_ref, wp_ref, wq_ref, w3_ref, out_ref, s_ref, z_ref):
    def widen(m, _):
        part = x_ref[m].astype(F32)
        s_ref[pl.ds(pl.multiple_of(m * NBIN, NBIN), NBIN), :] = part[:, :BLK]
        s_ref[pl.ds(pl.multiple_of((MSRC + m) * NBIN, NBIN), NBIN), :] = part[:, BLK:]
        return 0

    lax.fori_loop(0, MSRC, widen, 0, unroll=4)

    def load(b):
        return s_ref[pl.ds(b, 2 * MSRC, stride=NBIN), :].astype(BF)

    def pair(i, _):
        both = jnp.concatenate([load(2 * i), load(2 * i + 1)], axis=1)
        first = dot(w1_ref[...], both)
        first = first[: 2 * N1] + first[2 * N1 :]
        c, s = tw_ref[0], tw_ref[1]
        halves = []
        for u in range(2):
            re = first[:N1, u * BLK : (u + 1) * BLK]
            im = first[N1:, u * BLK : (u + 1) * BLK]
            halves.append(jnp.concatenate([re * c + im * s, im * c - re * s], axis=1).astype(BF))
        spectrum = dot(jnp.concatenate(halves, axis=0), wp_ref[...])
        spectrum = spectrum[:, : 2 * BLK] + spectrum[:, 2 * BLK :]
        products = []
        for u in range(2):
            xr = spectrum[u * N1 : (u + 1) * N1, :BLK]
            xi = spectrum[u * N1 : (u + 1) * N1, BLK:]
            hr = h_ref[2 * i + u, :, :BLK]
            hi = h_ref[2 * i + u, :, BLK:]
            products.append(jnp.concatenate([xr * hr - xi * hi, xr * hi + xi * hr], axis=1).astype(BF))
        back = dot(jnp.concatenate(products, axis=0), wq_ref[...])
        back = back[:, : 2 * BLK] + back[:, 2 * BLK :]
        columns = []
        for u in range(2):
            re = back[u * N1 : (u + 1) * N1, :BLK]
            im = back[u * N1 : (u + 1) * N1, BLK:]
            columns.append(jnp.concatenate([re * c - im * s, im * c + re * s], axis=0).astype(BF))
        last = dot(w3_ref[...], jnp.concatenate(columns, axis=1))
        last = last[: 2 * MOUT] + last[2 * MOUT :]
        for u in range(2):
            z_ref[pl.ds(2 * i + u, 2 * MOUT, stride=NBIN), :] = last[:, u * BLK : (u + 1) * BLK]
        return 0

    lax.fori_loop(0, NBIN // 2, pair, 0)

    n_az = out_ref.shape[0]
    rows = MOUT // n_az * NBIN

    def narrow(a, _):
        for part in range(2):
            o = pl.multiple_of((part * n_az + a) * rows, rows)
            out_ref[a, part * rows : (part + 1) * rows, :] = z_ref[pl.ds(o, rows), :].astype(BF)
        return 0

    lax.fori_loop(0, n_az, narrow, 0)


def focus(x, spectrum, n_az, n_rg):
    order = source_order(n_az, n_rg)
    w1 = left_table(angles(np.arange(N1), order, N1), -1.0)
    wp = right_table(angles(np.arange(BLK), np.arange(BLK), BLK), -1.0)
    wq = right_table(angles(np.arange(BLK), np.arange(BLK), BLK), 1.0)
    w3 = left_table(angles(np.arange(MOUT), np.arange(N1), N1), 1.0)
    vmem = pl.BlockSpec(memory_space=pltpu.VMEM)
    return pl.pallas_call(
        focus_kernel,
        out_shape=jax.ShapeDtypeStruct((n_az, 2 * MOUT // n_az * NBIN, BLK), BF),
        in_specs=[vmem] * 7,
        out_specs=vmem,
        scratch_shapes=[
            pltpu.VMEM((2 * MSRC * NBIN, BLK), F32),
            pltpu.VMEM((2 * MOUT * NBIN, BLK), F32),
        ],
        compiler_params=pltpu.CompilerParams(vmem_limit_bytes=VMEM),
        cost_estimate=pl.CostEstimate(flops=6_000_000_000, bytes_accessed=10_000_000, transcendentals=0),
    )(x, spectrum, jnp.asarray(w1), jnp.asarray(twiddle()), jnp.asarray(wp), jnp.asarray(wq), jnp.asarray(w3))


def turn_kernel(y_ref, out_ref):
    n_az, rows, _ = y_ref.shape
    for i in range(rows // NBIN):
        part = y_ref[:, i * NBIN : (i + 1) * NBIN, :].reshape(n_az * NBIN, BLK)
        out_ref[0, i * BLK : (i + 1) * BLK, :] = part.astype(F32).T


def turn(y):
    n_az, rows, _ = y.shape
    steps = 8
    return pl.pallas_call(
        turn_kernel,
        grid=(steps,),
        out_shape=jax.ShapeDtypeStruct((2, rows // NBIN // 2 * BLK, n_az * NBIN), F32),
        in_specs=[pl.BlockSpec((n_az, rows // steps, BLK), lambda g: (0, g, 0))],
        out_specs=pl.BlockSpec(
            (1, rows // NBIN // steps * BLK, n_az * NBIN), lambda g: (g // (steps // 2), g % (steps // 2), 0)
        ),
        cost_estimate=pl.CostEstimate(flops=0, bytes_accessed=6_000_000, transcendentals=0),
    )(y)


def own_taps(az_filter, az_lengths):
    first = lax.axis_index("az") * NBIN
    taps = lax.dynamic_slice_in_dim(az_filter, first, NBIN, 2)
    lengths = lax.dynamic_slice_in_dim(az_lengths, first, NBIN, 0)
    kept = jnp.arange(taps.shape[1])[:, None] < lengths[None, :]
    taps = jnp.where(kept[None], taps, jnp.zeros((), BF))
    return taps.transpose(2, 0, 1).reshape(NBIN, 2 * MFIL, BLK)


def per_device(raw, range_filter, mig_offsets, mig_widths, mig_coefs, az_filter, az_lengths):
    n_az, n_rg = lax.axis_size("az"), lax.axis_size("rg")
    moved = compress(raw, range_filter, mig_offsets, mig_widths, mig_coefs)
    moved = moved.reshape(n_rg * n_az, NBIN, 2 * BLK)
    x = lax.all_to_all(moved, ("rg", "az"), 0, 0, tiled=True)
    spectrum = filter_spectrum(own_taps(az_filter, az_lengths))
    y = focus(x, spectrum, n_az, n_rg)
    y = lax.all_to_all(y, "az", 0, 0, tiled=True)
    return turn(y)


def solution(mesh):
    return jax.shard_map(
        per_device,
        mesh=mesh,
        in_specs=(P(None, ("az", "rg"), None), P(), P(), P(), P(), P(None, None, "rg"), P("rg")),
        out_specs=P(None, "az", "rg"),
        check_vma=False,
    )
```

```python
import functools
import math

import jax
import jax.numpy as jnp
import numpy as np
from jax import lax
from jax.experimental import pallas as pl
from jax.experimental.pallas import tpu as pltpu
from jax.sharding import PartitionSpec as P

BF = jnp.bfloat16
F32 = jnp.float32
BLK = 128
TAPB = 32
NBLK = 32
NOUT = 33
NSAMP = 65
N1 = 160
MSRC = 128
MOUT = 128
MFIL = 32
NBIN = 32
VMEM = 60 * 1024 * 1024
GROUPS = (11, 11, 11)
EARLY = 8
NT = (((1,), (1,)), ((), ()))


def dot(a, b):
    return jnp.dot(a, b, preferred_element_type=F32)


def compress_kernel(
    off_hbm, wid_hbm, filt_ref, coef_ref, raw_hbm, out_ref, x_ref, g_ref, c_ref, f_ref, r_ref, w_ref, off_ref, wid_ref, sems, small
):
    def block_copy(s):
        o = pl.multiple_of(s * BLK, BLK)
        return pltpu.make_async_copy(raw_hbm.at[:, :, pl.ds(o, BLK)], x_ref.at[:, pl.ds(o, BLK), :], sems.at[s])

    copies = [
        pltpu.make_async_copy(off_hbm, off_ref, small.at[0]),
        pltpu.make_async_copy(wid_hbm, wid_ref, small.at[1]),
    ]

    def start(s, _):
        block_copy(s).start()
        return 0

    lax.fori_loop(0, NSAMP, start, 0)
    for copy in copies:
        copy.start()

    filt = filt_ref[...].astype(F32)
    for j in range(TAPB):
        for part in range(2):
            f_ref[part, j : j + 1, :] = filt[part : part + 1, j * BLK : (j + 1) * BLK]
    row_of = lax.broadcasted_iota(jnp.int32, (BLK, BLK), 0)
    col_of = lax.broadcasted_iota(jnp.int32, (BLK, BLK), 1)
    exchange = jnp.where(row_of + col_of == BLK - 1, 1.0, 0.0).astype(BF)
    r_ref[...] = jnp.zeros_like(r_ref)
    for part in range(2):
        r_ref[part, 1 : 1 + TAPB, :] = dot(f_ref[part].astype(BF), exchange)

    def table(j):
        o = j * 2 * BLK

        def spread(part):
            row = jnp.concatenate([r_ref[part, j + 1 : j + 2, :], r_ref[part, j : j + 1, :]], axis=1)
            wide = jnp.broadcast_to(row, (BLK, 2 * BLK))
            return pltpu.roll(wide, BLK + 1, 1, stride=1, stride_axis=0)[:, :BLK]

        re = spread(0)
        im = spread(1)
        g_ref[o : o + BLK, 0:BLK] = re.astype(BF)
        g_ref[o : o + BLK, BLK:] = im.astype(BF)
        g_ref[o + BLK : o + 2 * BLK, 0:BLK] = (-im).astype(BF)
        g_ref[o + BLK : o + 2 * BLK, BLK:] = re.astype(BF)

    def finish(s, _):
        block_copy(s).wait()
        return 0

    lane = lax.broadcasted_iota(jnp.int32, (1, BLK), 1)

    def migrate(b):
        row = jnp.where(lane < wid_ref[b], w_ref[b : b + 1, :], 0.0)
        row = jnp.concatenate([row, jnp.zeros_like(row)], axis=1)
        row = pltpu.roll(jnp.broadcast_to(row, (8, 2 * BLK)), off_ref[b], 1)[0:1]
        wide = jnp.broadcast_to(row, (BLK, 2 * BLK))
        band = pltpu.roll(wide, 0, 1, stride=1, stride_axis=0).astype(BF)
        window = jnp.concatenate([c_ref[b], c_ref[b + 1]], axis=1)
        moved = lax.dot_general(band, window, NT, preferred_element_type=F32)
        out_ref[b * BLK : (b + 1) * BLK, :] = moved.astype(BF)

    w_ref[:, 0 : coef_ref.shape[1]] = coef_ref[...].astype(F32)
    for copy in copies:
        copy.wait()
    for j in range(EARLY):
        table(j)
    lax.fori_loop(0, NSAMP, finish, 0)

    done, moved = 0, 0
    for count in GROUPS:
        rows = count * BLK
        acc = jnp.zeros((rows, 2 * BLK), F32)
        for j in range(NOUT):
            r0 = (done + j) * BLK
            both = jnp.concatenate([x_ref[0, r0 : r0 + rows, :], x_ref[1, r0 : r0 + rows, :]], axis=1)
            acc = acc + dot(both, g_ref[j * 2 * BLK : (j + 1) * 2 * BLK, :])
            if done == 0 and j + EARLY < NOUT:
                table(j + EARLY)
            if j % 2 == 1 and moved < done - 1:
                migrate(moved)
                moved += 1
        out = acc.astype(BF)
        for b in range(count):
            part = out[b * BLK : (b + 1) * BLK]
            c_ref[done + b, 0:BLK, :] = part[:, :BLK]
            c_ref[done + b, BLK:, :] = part[:, BLK:]
        done += count
    for b in range(moved, NBLK):
        migrate(b)


def compress(raw, range_filter, offsets, widths, coefs):
    vmem = pl.BlockSpec(memory_space=pltpu.VMEM)
    hbm = pl.BlockSpec(memory_space=pltpu.HBM)
    return pl.pallas_call(
        compress_kernel,
        out_shape=jax.ShapeDtypeStruct((NBLK * BLK, 2 * BLK), BF),
        in_specs=[hbm, hbm, vmem, vmem, hbm],
        out_specs=vmem,
        scratch_shapes=[
            pltpu.VMEM((2, NSAMP * BLK, BLK), BF),
            pltpu.VMEM((NOUT * 2 * BLK, 2 * BLK), BF),
            pltpu.VMEM((NOUT, 2 * BLK, BLK), BF),
            pltpu.VMEM((2, TAPB, BLK), F32),
            pltpu.VMEM((2, TAPB + 8, BLK), F32),
            pltpu.VMEM((NBLK, BLK), F32),
            pltpu.SMEM((NBLK,), jnp.int32),
            pltpu.SMEM((NBLK,), jnp.int32),
            pltpu.SemaphoreType.DMA((NSAMP,)),
            pltpu.SemaphoreType.DMA((2,)),
        ],
        compiler_params=pltpu.CompilerParams(vmem_limit_bytes=VMEM),
        cost_estimate=pl.CostEstimate(flops=18_300_000_000, bytes_accessed=8_000_000, transcendentals=0),
    )(offsets, widths, range_filter, coefs, raw)


def split(table):
    hi = table.astype(np.float32).astype(jnp.bfloat16)
    lo = (table - hi.astype(np.float64)).astype(np.float32).astype(jnp.bfloat16)
    return hi, lo


def angles(rows, cols, period):
    return 2.0 * np.pi * (np.outer(rows, cols) % period) / period


def complex_table(theta, sign):
    c, s = np.cos(theta), sign * np.sin(theta)
    return split(np.block([[c, -s], [s, c]]))


def stacked_table(theta, sign):
    return np.concatenate(complex_table(theta, sign), axis=0)


def left_table(theta, sign):
    hi, lo = complex_table(theta, sign)
    return np.concatenate([hi, hi, lo], axis=1)


def right_table(theta, sign):
    hi, lo = complex_table(theta, sign)
    return np.concatenate([hi.T, hi.T, lo.T], axis=0)


def parts(value):
    hi = value.astype(BF)
    return hi, (value - hi.astype(F32)).astype(BF)


def source_order(n_az, n_rg):
    s = np.arange(n_az * n_rg)
    return (s % n_az) * n_rg + s // n_az


def twiddle():
    theta = angles(np.arange(N1), np.arange(BLK), N1 * BLK)
    return np.stack([np.cos(theta), np.sin(theta)]).astype(np.float32)


def filter_kernel(taps_ref, w1_ref, tw_ref, wp_ref, h_ref):
    def pair(i, _):
        both = jnp.concatenate([taps_ref[2 * i], taps_ref[2 * i + 1]], axis=1)
        first = dot(w1_ref[...], both)
        first = first[: 2 * N1] + first[2 * N1 :]
        for u in range(2):
            re = first[:N1, u * BLK : (u + 1) * BLK]
            im = first[N1:, u * BLK : (u + 1) * BLK]
            c, s = tw_ref[0], tw_ref[1]
            hi, lo = parts(jnp.concatenate([re * c - im * s, im * c + re * s], axis=1))
            second = dot(jnp.concatenate([hi, lo, hi], axis=1), wp_ref[...])
            h_ref[2 * i + u] = second * (1.0 / (N1 * BLK))
        return 0

    lax.fori_loop(0, NBIN // 2, pair, 0)


def filter_spectrum(taps):
    w1 = stacked_table(angles(np.arange(N1), np.arange(MFIL), N1), 1.0)
    wp = right_table(angles(np.arange(BLK), np.arange(BLK), BLK), 1.0)
    vmem = pl.BlockSpec(memory_space=pltpu.VMEM)
    return pl.pallas_call(
        filter_kernel,
        out_shape=jax.ShapeDtypeStruct((NBIN, N1, 2 * BLK), F32),
        in_specs=[vmem] * 4,
        out_specs=vmem,
        compiler_params=pltpu.CompilerParams(vmem_limit_bytes=VMEM),
        cost_estimate=pl.CostEstimate(flops=4_000_000_000, bytes_accessed=8_000_000, transcendentals=0),
    )(taps, jnp.asarray(w1), jnp.asarray(twiddle()), jnp.asarray(wp))


def focus_kernel(x_ref, h_hbm, w1_ref, tw_ref, wp_ref, wq_ref, w3_ref, out_ref, s_ref, z_ref, h_ref, *scratch):
    stage1, stage2, stage3, sem = scratch[0:2], scratch[2:4], scratch[4:6], scratch[6]
    copy = pltpu.make_async_copy(h_hbm, h_ref, sem)
    copy.start()

    def widen(m, _):
        part = x_ref[m].astype(F32)
        s_ref[pl.ds(pl.multiple_of(m * NBIN, NBIN), NBIN), :] = part[:, :BLK]
        s_ref[pl.ds(pl.multiple_of((MSRC + m) * NBIN, NBIN), NBIN), :] = part[:, BLK:]
        return 0

    lax.fori_loop(0, MSRC, widen, 0, unroll=8)
    copy.wait()

    def load(b):
        return s_ref[pl.ds(b, 2 * MSRC, stride=NBIN), :].astype(BF)

    def coarse(i, to):
        both = jnp.concatenate([load(2 * i), load(2 * i + 1)], axis=1)
        first = dot(w1_ref[...], both)
        first = first[: 2 * N1] + first[2 * N1 :]
        c, s = tw_ref[0], tw_ref[1]
        for u in range(2):
            rows = slice(u * N1, (u + 1) * N1)
            re = first[:N1, u * BLK : (u + 1) * BLK]
            im = first[N1:, u * BLK : (u + 1) * BLK]
            to[rows, 0:BLK], to[rows, 2 * BLK : 3 * BLK] = parts(re * c + im * s)
            to[rows, BLK : 2 * BLK], to[rows, 3 * BLK :] = parts(im * c - re * s)

    def wide(at):
        return jnp.concatenate([at[...], at[:, : 2 * BLK]], axis=1)

    def fine(i, at, to):
        spectrum = dot(wide(at), wp_ref[...])
        for u in range(2):
            rows = slice(u * N1, (u + 1) * N1)
            xr = spectrum[rows, :BLK]
            xi = spectrum[rows, BLK:]
            hr = h_ref[2 * i + u, :, :BLK]
            hi = h_ref[2 * i + u, :, BLK:]
            to[rows, 0:BLK], to[rows, 2 * BLK : 3 * BLK] = parts(xr * hr - xi * hi)
            to[rows, BLK : 2 * BLK], to[rows, 3 * BLK :] = parts(xr * hi + xi * hr)

    def fine_back(at, to):
        back = dot(wide(at), wq_ref[...])
        c, s = tw_ref[0], tw_ref[1]
        for u in range(2):
            lanes = slice(u * BLK, (u + 1) * BLK)
            re = back[u * N1 : (u + 1) * N1, :BLK]
            im = back[u * N1 : (u + 1) * N1, BLK:]
            to[0:N1, lanes], to[2 * N1 : 3 * N1, lanes] = parts(re * c - im * s)
            to[N1 : 2 * N1, lanes], to[3 * N1 :, lanes] = parts(im * c + re * s)

    def coarse_back(i, at):
        last = dot(w3_ref[...], jnp.concatenate([at[...], at[: 2 * N1, :]], axis=0))
        for u in range(2):
            z_ref[pl.ds(2 * i + u, 2 * MOUT, stride=NBIN), :] = last[:, u * BLK : (u + 1) * BLK]

    pairs = NBIN // 2

    def step(q, parity, first, last):
        if first <= 3 <= last:
            coarse_back(q - 3, stage3[1 - parity])
        if first <= 2 <= last:
            fine_back(stage2[parity], stage3[parity])
        if first <= 1 <= last:
            fine(q - 1, stage1[1 - parity], stage2[1 - parity])
        if first <= 0 <= last:
            coarse(q, stage1[parity])

    for q in range(3):
        step(q, q % 2, 0, q)

    def two(i, _):
        step(3 + 2 * i, 1, 0, 3)
        step(4 + 2 * i, 0, 0, 3)
        return 0

    lax.fori_loop(0, (pairs - 4) // 2, two, 0)
    step(pairs - 1, (pairs - 1) % 2, 0, 3)
    for q in range(pairs, pairs + 3):
        step(q, q % 2, q - pairs + 1, 3)

    n_az = out_ref.shape[0]
    rows = MOUT // n_az * NBIN

    def narrow(a, _):
        for part in range(2):
            o = pl.multiple_of((part * n_az + a) * rows, rows)
            out_ref[a, part * rows : (part + 1) * rows, :] = z_ref[pl.ds(o, rows), :].astype(BF)
        return 0

    lax.fori_loop(0, n_az, narrow, 0)


def focus(x, spectrum, n_az, n_rg):
    order = source_order(n_az, n_rg)
    w1 = stacked_table(angles(np.arange(N1), order, N1), -1.0)
    wp = right_table(angles(np.arange(BLK), np.arange(BLK), BLK), -1.0)
    wq = right_table(angles(np.arange(BLK), np.arange(BLK), BLK), 1.0)
    w3 = left_table(angles(np.arange(MOUT), np.arange(N1), N1), 1.0)
    vmem = pl.BlockSpec(memory_space=pltpu.VMEM)
    return pl.pallas_call(
        focus_kernel,
        out_shape=jax.ShapeDtypeStruct((n_az, 2 * MOUT // n_az * NBIN, BLK), BF),
        in_specs=[vmem, pl.BlockSpec(memory_space=pl.ANY)] + [vmem] * 5,
        out_specs=vmem,
        scratch_shapes=[
            pltpu.VMEM((2 * MSRC * NBIN, BLK), F32),
            pltpu.VMEM((2 * MOUT * NBIN, BLK), F32),
            pltpu.VMEM((NBIN, N1, 2 * BLK), F32),
            *[pltpu.VMEM((2 * N1, 4 * BLK), BF)] * 4,
            *[pltpu.VMEM((4 * N1, 2 * BLK), BF)] * 2,
            pltpu.SemaphoreType.DMA(()),
        ],
        compiler_params=pltpu.CompilerParams(vmem_limit_bytes=VMEM),
        cost_estimate=pl.CostEstimate(flops=6_000_000_000, bytes_accessed=10_000_000, transcendentals=0),
    )(x, spectrum, jnp.asarray(w1), jnp.asarray(twiddle()), jnp.asarray(wp), jnp.asarray(wq), jnp.asarray(w3))


def turn_kernel(y_ref, out_ref):
    n_az, rows, _ = y_ref.shape
    row_of = lax.broadcasted_iota(jnp.int32, (BLK, BLK), 0)
    col_of = lax.broadcasted_iota(jnp.int32, (BLK, BLK), 1)
    unit = jnp.where(row_of == col_of, 1.0, 0.0).astype(BF)
    for i in range(rows // NBIN):
        part = y_ref[:, i * NBIN : (i + 1) * NBIN, :].reshape(n_az * NBIN, BLK)
        out_ref[0, i * BLK : (i + 1) * BLK, :] = lax.dot_general(unit, part, NT, preferred_element_type=F32)


def turn(y):
    n_az, rows, _ = y.shape
    steps = 2
    return pl.pallas_call(
        turn_kernel,
        grid=(steps,),
        out_shape=jax.ShapeDtypeStruct((2, rows // NBIN // 2 * BLK, n_az * NBIN), F32),
        in_specs=[pl.BlockSpec((n_az, rows // steps, BLK), lambda g: (0, g, 0))],
        out_specs=pl.BlockSpec(
            (1, rows // NBIN // steps * BLK, n_az * NBIN), lambda g: (g // (steps // 2), g % (steps // 2), 0)
        ),
        compiler_params=pltpu.CompilerParams(vmem_limit_bytes=VMEM),
        cost_estimate=pl.CostEstimate(flops=0, bytes_accessed=6_000_000, transcendentals=0),
    )(y)


def own_taps(az_filter, az_lengths):
    first = lax.axis_index("az") * NBIN
    taps = lax.dynamic_slice_in_dim(az_filter, first, NBIN, 2)
    lengths = lax.dynamic_slice_in_dim(az_lengths, first, NBIN, 0)
    kept = jnp.arange(taps.shape[1])[:, None] < lengths[None, :]
    taps = jnp.where(kept[None], taps, jnp.zeros((), BF))
    return taps.transpose(2, 0, 1).reshape(NBIN, 2 * MFIL, BLK)


def per_device(raw, range_filter, mig_offsets, mig_widths, mig_coefs, az_filter, az_lengths):
    n_az, n_rg = lax.axis_size("az"), lax.axis_size("rg")
    moved = compress(raw, range_filter, mig_offsets, mig_widths, mig_coefs)
    moved = moved.reshape(n_rg * n_az, NBIN, 2 * BLK)
    x = lax.all_to_all(moved, ("rg", "az"), 0, 0, tiled=True)
    spectrum = filter_spectrum(own_taps(az_filter, az_lengths))
    y = focus(x, spectrum, n_az, n_rg)
    y = lax.all_to_all(y, "az", 0, 0, tiled=True)
    return turn(y)


def solution(mesh):
    return jax.shard_map(
        per_device,
        mesh=mesh,
        in_specs=(P(None, ("az", "rg"), None), P(), P(), P(), P(), P(None, None, "rg"), P("rg")),
        out_specs=P(None, "az", "rg"),
        check_vma=False,
    )
```

```python
import functools
import math

import jax
import jax.numpy as jnp
import numpy as np
from jax import lax
from jax.experimental import pallas as pl
from jax.experimental.pallas import tpu as pltpu
from jax.sharding import PartitionSpec as P

BF = jnp.bfloat16
F32 = jnp.float32
BLK = 128
TAPB = 32
NBLK = 32
NOUT = 33
NSAMP = 65
N1 = 160
MSRC = 128
MOUT = 128
MFIL = 32
NBIN = 32
PIECES = 4
SIDE = 2
PITCH = 40
VMEM = 60 * 1024 * 1024
GROUPS = (11, 11, 11)
EARLY = 8
NT = (((1,), (1,)), ((), ()))


def dot(a, b):
    return jnp.dot(a, b, preferred_element_type=F32)


def compress_kernel(
    off_hbm, wid_hbm, filt_ref, coef_ref, raw_hbm, out_ref, x_ref, g_ref, c_ref, f_ref, r_ref, w_ref, off_ref, wid_ref, sems, small
):
    def block_copy(s):
        o = pl.multiple_of(s * BLK, BLK)
        return pltpu.make_async_copy(raw_hbm.at[:, :, pl.ds(o, BLK)], x_ref.at[:, pl.ds(o, BLK), :], sems.at[s])

    copies = [
        pltpu.make_async_copy(off_hbm, off_ref, small.at[0]),
        pltpu.make_async_copy(wid_hbm, wid_ref, small.at[1]),
    ]

    def start(s, _):
        block_copy(s).start()
        return 0

    lax.fori_loop(0, NSAMP, start, 0)
    for copy in copies:
        copy.start()

    filt = filt_ref[...].astype(F32)
    for j in range(TAPB):
        for part in range(2):
            f_ref[part, j : j + 1, :] = filt[part : part + 1, j * BLK : (j + 1) * BLK]
    row_of = lax.broadcasted_iota(jnp.int32, (BLK, BLK), 0)
    col_of = lax.broadcasted_iota(jnp.int32, (BLK, BLK), 1)
    exchange = jnp.where(row_of + col_of == BLK - 1, 1.0, 0.0).astype(BF)
    r_ref[...] = jnp.zeros_like(r_ref)
    for part in range(2):
        r_ref[part, 1 : 1 + TAPB, :] = dot(f_ref[part].astype(BF), exchange)

    def table(j):
        o = j * 2 * BLK

        def spread(part):
            row = jnp.concatenate([r_ref[part, j + 1 : j + 2, :], r_ref[part, j : j + 1, :]], axis=1)
            wide = jnp.broadcast_to(row, (BLK, 2 * BLK))
            return pltpu.roll(wide, BLK + 1, 1, stride=1, stride_axis=0)[:, :BLK]

        re = spread(0)
        im = spread(1)
        g_ref[o : o + BLK, 0:BLK] = re.astype(BF)
        g_ref[o : o + BLK, BLK:] = im.astype(BF)
        g_ref[o + BLK : o + 2 * BLK, 0:BLK] = (-im).astype(BF)
        g_ref[o + BLK : o + 2 * BLK, BLK:] = re.astype(BF)

    def finish(s, _):
        block_copy(s).wait()
        return 0

    lane = lax.broadcasted_iota(jnp.int32, (1, BLK), 1)

    def migrate(b):
        row = jnp.where(lane < wid_ref[b], w_ref[b : b + 1, :], 0.0)
        row = jnp.concatenate([row, jnp.zeros_like(row)], axis=1)
        row = pltpu.roll(jnp.broadcast_to(row, (8, 2 * BLK)), off_ref[b], 1)[0:1]
        wide = jnp.broadcast_to(row, (BLK, 2 * BLK))
        band = pltpu.roll(wide, 0, 1, stride=1, stride_axis=0).astype(BF)
        window = jnp.concatenate([c_ref[b], c_ref[b + 1]], axis=1)
        moved = lax.dot_general(band, window, NT, preferred_element_type=F32)
        out_ref[b * BLK : (b + 1) * BLK, :] = moved.astype(BF)

    w_ref[:, 0 : coef_ref.shape[1]] = coef_ref[...].astype(F32)
    for copy in copies:
        copy.wait()
    for j in range(EARLY):
        table(j)
    lax.fori_loop(0, NSAMP, finish, 0)

    done, moved = 0, 0
    for count in GROUPS:
        rows = count * BLK
        acc = jnp.zeros((rows, 2 * BLK), F32)
        for j in range(NOUT):
            r0 = (done + j) * BLK
            both = jnp.concatenate([x_ref[0, r0 : r0 + rows, :], x_ref[1, r0 : r0 + rows, :]], axis=1)
            acc = acc + dot(both, g_ref[j * 2 * BLK : (j + 1) * 2 * BLK, :])
            if done == 0 and j + EARLY < NOUT:
                table(j + EARLY)
            if j % 2 == 1 and moved < done - 1:
                migrate(moved)
                moved += 1
        out = acc.astype(BF)
        for b in range(count):
            part = out[b * BLK : (b + 1) * BLK]
            c_ref[done + b, 0:BLK, :] = part[:, :BLK]
            c_ref[done + b, BLK:, :] = part[:, BLK:]
        done += count
    for b in range(moved, NBLK):
        migrate(b)


def compress(raw, range_filter, offsets, widths, coefs):
    vmem = pl.BlockSpec(memory_space=pltpu.VMEM)
    hbm = pl.BlockSpec(memory_space=pltpu.HBM)
    return pl.pallas_call(
        compress_kernel,
        out_shape=jax.ShapeDtypeStruct((NBLK * BLK, 2 * BLK), BF),
        in_specs=[hbm, hbm, vmem, vmem, hbm],
        out_specs=vmem,
        scratch_shapes=[
            pltpu.VMEM((2, NSAMP * BLK, BLK), BF),
            pltpu.VMEM((NOUT * 2 * BLK, 2 * BLK), BF),
            pltpu.VMEM((NOUT, 2 * BLK, BLK), BF),
            pltpu.VMEM((2, TAPB, BLK), F32),
            pltpu.VMEM((2, TAPB + 8, BLK), F32),
            pltpu.VMEM((NBLK, BLK), F32),
            pltpu.SMEM((NBLK,), jnp.int32),
            pltpu.SMEM((NBLK,), jnp.int32),
            pltpu.SemaphoreType.DMA((NSAMP,)),
            pltpu.SemaphoreType.DMA((2,)),
        ],
        compiler_params=pltpu.CompilerParams(vmem_limit_bytes=VMEM),
        cost_estimate=pl.CostEstimate(flops=18_300_000_000, bytes_accessed=8_000_000, transcendentals=0),
    )(offsets, widths, range_filter, coefs, raw)


def split(table):
    hi = table.astype(np.float32).astype(jnp.bfloat16)
    lo = (table - hi.astype(np.float64)).astype(np.float32).astype(jnp.bfloat16)
    return hi, lo


def angles(rows, cols, period):
    return 2.0 * np.pi * (np.outer(rows, cols) % period) / period


def complex_table(theta, sign):
    c, s = np.cos(theta), sign * np.sin(theta)
    return split(np.block([[c, -s], [s, c]]))


def stacked_table(theta, sign):
    return np.concatenate(complex_table(theta, sign), axis=0)


def left_table(theta, sign):
    hi, lo = complex_table(theta, sign)
    return np.concatenate([hi, hi, lo], axis=1)


def right_table(theta, sign):
    hi, lo = complex_table(theta, sign)
    return np.concatenate([hi.T, hi.T, lo.T], axis=0)


def parts(value):
    hi = value.astype(BF)
    return hi, (value - hi.astype(F32)).astype(BF)


def source_order(n_az, n_rg):
    s = np.arange(n_az * n_rg)
    return (s % n_az) * n_rg + s // n_az


def twiddle():
    theta = angles(np.arange(N1), np.arange(BLK), N1 * BLK)
    return np.stack([np.cos(theta), np.sin(theta)]).astype(np.float32)


def filter_kernel(taps_ref, w1_ref, tw_ref, wp_ref, h_ref):
    def pair(i, _):
        both = jnp.concatenate([taps_ref[2 * i], taps_ref[2 * i + 1]], axis=1)
        first = dot(w1_ref[...], both)
        first = first[: 2 * N1] + first[2 * N1 :]
        for u in range(2):
            re = first[:N1, u * BLK : (u + 1) * BLK]
            im = first[N1:, u * BLK : (u + 1) * BLK]
            c, s = tw_ref[0], tw_ref[1]
            hi, lo = parts(jnp.concatenate([re * c - im * s, im * c + re * s], axis=1))
            second = dot(jnp.concatenate([hi, lo, hi], axis=1), wp_ref[...])
            h_ref[2 * i + u] = second * (1.0 / (N1 * BLK))
        return 0

    lax.fori_loop(0, NBIN // 2, pair, 0)


def filter_spectrum(taps):
    w1 = stacked_table(angles(np.arange(N1), np.arange(MFIL), N1), 1.0)
    wp = right_table(angles(np.arange(BLK), np.arange(BLK), BLK), 1.0)
    vmem = pl.BlockSpec(memory_space=pltpu.VMEM)
    return pl.pallas_call(
        filter_kernel,
        out_shape=jax.ShapeDtypeStruct((NBIN, N1, 2 * BLK), F32),
        in_specs=[vmem] * 4,
        out_specs=vmem,
        compiler_params=pltpu.CompilerParams(vmem_limit_bytes=VMEM),
        cost_estimate=pl.CostEstimate(flops=4_000_000_000, bytes_accessed=8_000_000, transcendentals=0),
    )(taps, jnp.asarray(w1), jnp.asarray(twiddle()), jnp.asarray(wp))


def focus_kernel(x_hbm, h_hbm, w1_hbm, tw_hbm, wp_hbm, wq_hbm, w3_hbm, out_hbm, *scratch):
    x_ref, h_ref, w1_ref, tw_ref, wp_ref, wq_ref, w3_ref, out_ref, s_ref, z_ref = scratch[:10]
    stage1, stage2, stage3 = scratch[10:12], scratch[12:14], scratch[14:16]
    x_sems, t_sems, o_sems = scratch[16:]
    piece = MSRC // PIECES
    arriving = []
    for i in range(PIECES):
        part = pl.ds(i * piece, piece)
        arriving.append(pltpu.make_async_copy(x_hbm.at[part], x_ref.at[part], x_sems.at[i]))
    tables = [(w1_hbm, w1_ref), (tw_hbm, tw_ref), (h_hbm, h_ref), (wp_hbm, wp_ref), (wq_hbm, wq_ref), (w3_hbm, w3_ref)]
    tables = [pltpu.make_async_copy(src, dst, t_sems.at[i]) for i, (src, dst) in enumerate(tables)]
    for copy in arriving + tables:
        copy.start()

    def widen(m, _):
        part = x_ref[m].astype(F32)
        s_ref[pl.ds(pl.multiple_of(m * PITCH, 8), NBIN), :] = part[:, :BLK]
        s_ref[pl.ds(pl.multiple_of((MSRC + m) * PITCH, 8), NBIN), :] = part[:, BLK:]
        return 0

    for i in range(PIECES):
        arriving[i].wait()
        lax.fori_loop(i * piece, (i + 1) * piece, widen, 0, unroll=8)
    for copy in tables:
        copy.wait()

    def load(b):
        return s_ref[pl.ds(b, 2 * MSRC, stride=PITCH), :].astype(BF)

    def coarse(i, to):
        both = jnp.concatenate([load(SIDE * i + u) for u in range(SIDE)], axis=1)
        first = dot(w1_ref[...], both)
        first = first[: 2 * N1] + first[2 * N1 :]
        c, s = tw_ref[0], tw_ref[1]
        for u in range(SIDE):
            rows = slice(u * N1, (u + 1) * N1)
            re = first[:N1, u * BLK : (u + 1) * BLK]
            im = first[N1:, u * BLK : (u + 1) * BLK]
            to[rows, 0:BLK], to[rows, 2 * BLK : 3 * BLK] = parts(re * c + im * s)
            to[rows, BLK : 2 * BLK], to[rows, 3 * BLK :] = parts(im * c - re * s)

    def wide(at):
        return jnp.concatenate([at[...], at[:, : 2 * BLK]], axis=1)

    def fine(i, at, to):
        spectrum = dot(wide(at), wp_ref[...])
        for u in range(SIDE):
            rows = slice(u * N1, (u + 1) * N1)
            xr = spectrum[rows, :BLK]
            xi = spectrum[rows, BLK:]
            hr = h_ref[SIDE * i + u, :, :BLK]
            hi = h_ref[SIDE * i + u, :, BLK:]
            to[rows, 0:BLK], to[rows, 2 * BLK : 3 * BLK] = parts(xr * hr - xi * hi)
            to[rows, BLK : 2 * BLK], to[rows, 3 * BLK :] = parts(xr * hi + xi * hr)

    def fine_back(at, to):
        back = dot(wide(at), wq_ref[...])
        c, s = tw_ref[0], tw_ref[1]
        for u in range(SIDE):
            lanes = slice(u * BLK, (u + 1) * BLK)
            re = back[u * N1 : (u + 1) * N1, :BLK]
            im = back[u * N1 : (u + 1) * N1, BLK:]
            to[0:N1, lanes], to[2 * N1 : 3 * N1, lanes] = parts(re * c - im * s)
            to[N1 : 2 * N1, lanes], to[3 * N1 :, lanes] = parts(im * c + re * s)

    def coarse_back(i, at):
        last = dot(w3_ref[...], jnp.concatenate([at[...], at[: 2 * N1, :]], axis=0))
        for u in range(SIDE):
            z_ref[pl.ds(SIDE * i + u, 2 * MOUT, stride=PITCH), :] = last[:, u * BLK : (u + 1) * BLK]

    pairs = NBIN // SIDE

    def step(q, parity, first, last):
        if first <= 3 <= last:
            coarse_back(q - 3, stage3[1 - parity])
        if first <= 2 <= last:
            fine_back(stage2[parity], stage3[parity])
        if first <= 1 <= last:
            fine(q - 1, stage1[1 - parity], stage2[1 - parity])
        if first <= 0 <= last:
            coarse(q, stage1[parity])

    for q in range(3):
        step(q, q % 2, 0, q)

    def two(i, _):
        step(3 + 2 * i, 1, 0, 3)
        step(4 + 2 * i, 0, 0, 3)
        return 0

    lax.fori_loop(0, (pairs - 4) // 2, two, 0)
    step(pairs - 1, (pairs - 1) % 2, 0, 3)
    for q in range(pairs, pairs + 3):
        step(q, q % 2, q - pairs + 1, 3)

    n_az = out_ref.shape[0]
    blocks = MOUT // n_az

    def leave(a):
        return pltpu.make_async_copy(out_ref.at[a], out_hbm.at[a], o_sems.at[a])

    def narrow(a, _):
        for part in range(2):
            for m in range(blocks):
                o = pl.multiple_of(((part * n_az + a) * blocks + m) * PITCH, 8)
                row = (part * blocks + m) * NBIN
                out_ref[a, row : row + NBIN, :] = z_ref[pl.ds(o, NBIN), :].astype(BF)
        leave(a).start()
        return 0

    lax.fori_loop(0, n_az, narrow, 0)

    def left(a, _):
        leave(a).wait()
        return 0

    lax.fori_loop(0, n_az, left, 0)


def focus(x, spectrum, n_az, n_rg):
    order = source_order(n_az, n_rg)
    w1 = stacked_table(angles(np.arange(N1), order, N1), -1.0)
    wp = right_table(angles(np.arange(BLK), np.arange(BLK), BLK), -1.0)
    wq = right_table(angles(np.arange(BLK), np.arange(BLK), BLK), 1.0)
    w3 = left_table(angles(np.arange(MOUT), np.arange(N1), N1), 1.0)
    hbm = pl.BlockSpec(memory_space=pltpu.HBM)
    out = (n_az, 2 * MOUT // n_az * NBIN, BLK)
    tables = [(w1, BF), (twiddle(), F32), (wp, BF), (wq, BF), (w3, BF)]
    return pl.pallas_call(
        focus_kernel,
        out_shape=jax.ShapeDtypeStruct(out, BF),
        in_specs=[hbm] * 7,
        out_specs=hbm,
        scratch_shapes=[
            pltpu.VMEM(x.shape, BF),
            pltpu.VMEM(spectrum.shape, F32),
            *[pltpu.VMEM(table.shape, kind) for table, kind in tables],
            pltpu.VMEM(out, BF),
            pltpu.VMEM((2 * MSRC * PITCH, BLK), F32),
            pltpu.VMEM((2 * MOUT * PITCH, BLK), F32),
            *[pltpu.VMEM((SIDE * N1, 4 * BLK), BF)] * 4,
            *[pltpu.VMEM((4 * N1, SIDE * BLK), BF)] * 2,
            pltpu.SemaphoreType.DMA((PIECES,)),
            pltpu.SemaphoreType.DMA((6,)),
            pltpu.SemaphoreType.DMA((n_az,)),
        ],
        compiler_params=pltpu.CompilerParams(vmem_limit_bytes=VMEM),
        cost_estimate=pl.CostEstimate(flops=6_000_000_000, bytes_accessed=10_000_000, transcendentals=0),
    )(x, spectrum, *[jnp.asarray(table) for table, _ in tables])


def turn_kernel(y_hbm, out_hbm, y_ref, out_ref, in_sems, out_sems):
    n_az, rows, _ = y_ref.shape
    piece = rows // PIECES
    arriving = []
    for i in range(PIECES):
        part = pl.ds(i * piece, piece)
        arriving.append(pltpu.make_async_copy(y_hbm.at[:, part, :], y_ref.at[:, part, :], in_sems.at[i]))
        arriving[-1].start()
    row_of = lax.broadcasted_iota(jnp.int32, (BLK, BLK), 0)
    col_of = lax.broadcasted_iota(jnp.int32, (BLK, BLK), 1)
    unit = jnp.where(row_of == col_of, 1.0, 0.0).astype(BF)
    leaving = []
    for i in range(PIECES):
        arriving[i].wait()
        for k in range(i * piece // NBIN, (i + 1) * piece // NBIN):
            part = y_ref[:, k * NBIN : (k + 1) * NBIN, :].reshape(n_az * NBIN, BLK)
            out_ref[k * BLK : (k + 1) * BLK, :] = lax.dot_general(unit, part, NT, preferred_element_type=F32)
        done = pl.ds(i * piece // NBIN * BLK, piece // NBIN * BLK)
        leaving.append(pltpu.make_async_copy(out_ref.at[done, :], out_hbm.at[done, :], out_sems.at[i]))
        leaving[-1].start()
    for copy in leaving:
        copy.wait()


def turn(y):
    n_az, rows, _ = y.shape
    out = (rows // NBIN * BLK, n_az * NBIN)
    hbm = pl.BlockSpec(memory_space=pltpu.HBM)
    image = pl.pallas_call(
        turn_kernel,
        out_shape=jax.ShapeDtypeStruct(out, F32),
        in_specs=[hbm],
        out_specs=hbm,
        scratch_shapes=[
            pltpu.VMEM(y.shape, BF),
            pltpu.VMEM(out, F32),
            pltpu.SemaphoreType.DMA((PIECES,)),
            pltpu.SemaphoreType.DMA((PIECES,)),
        ],
        compiler_params=pltpu.CompilerParams(vmem_limit_bytes=VMEM),
        cost_estimate=pl.CostEstimate(flops=0, bytes_accessed=6_000_000, transcendentals=0),
    )(y)
    return image.reshape(2, out[0] // 2, out[1])


def own_taps(az_filter, az_lengths):
    first = lax.axis_index("az") * NBIN
    taps = lax.dynamic_slice_in_dim(az_filter, first, NBIN, 2)
    lengths = lax.dynamic_slice_in_dim(az_lengths, first, NBIN, 0)
    kept = jnp.arange(taps.shape[1])[:, None] < lengths[None, :]
    taps = jnp.where(kept[None], taps, jnp.zeros((), BF))
    return taps.transpose(2, 0, 1).reshape(NBIN, 2 * MFIL, BLK)


def per_device(raw, range_filter, mig_offsets, mig_widths, mig_coefs, az_filter, az_lengths):
    n_az, n_rg = lax.axis_size("az"), lax.axis_size("rg")
    moved = compress(raw, range_filter, mig_offsets, mig_widths, mig_coefs)
    moved = moved.reshape(n_rg * n_az, NBIN, 2 * BLK)
    x = lax.all_to_all(moved, ("rg", "az"), 0, 0, tiled=True)
    spectrum = filter_spectrum(own_taps(az_filter, az_lengths))
    y = focus(x, spectrum, n_az, n_rg)
    y = lax.all_to_all(y, "az", 0, 0, tiled=True)
    return turn(y)


def solution(mesh):
    return jax.shard_map(
        per_device,
        mesh=mesh,
        in_specs=(P(None, ("az", "rg"), None), P(), P(), P(), P(), P(None, None, "rg"), P("rg")),
        out_specs=P(None, "az", "rg"),
        check_vma=False,
    )
```

```python
import functools
import math

import jax
import jax.numpy as jnp
import numpy as np
from jax import lax
from jax.experimental import pallas as pl
from jax.experimental.pallas import tpu as pltpu
from jax.sharding import PartitionSpec as P

BF = jnp.bfloat16
F32 = jnp.float32
BLK = 128
TAPB = 32
NBLK = 32
NOUT = 33
NSAMP = 65
N1 = 160
MSRC = 128
MOUT = 128
MFIL = 32
NBIN = 32
PIECES = 8
TURNS = 4
SIDE = 4
PITCH = 40
VMEM = 60 * 1024 * 1024
GROUPS = (11, 11, 11)
EARLY = 8
NT = (((1,), (1,)), ((), ()))


def dot(a, b):
    return jnp.dot(a, b, preferred_element_type=F32)


def compress_kernel(
    off_hbm, wid_hbm, filt_ref, coef_ref, raw_hbm, out_ref, x_ref, g_ref, c_ref, f_ref, r_ref, w_ref, off_ref, wid_ref, sems, small
):
    def block_copy(s):
        o = pl.multiple_of(s * BLK, BLK)
        return pltpu.make_async_copy(raw_hbm.at[:, :, pl.ds(o, BLK)], x_ref.at[:, pl.ds(o, BLK), :], sems.at[s])

    copies = [
        pltpu.make_async_copy(off_hbm, off_ref, small.at[0]),
        pltpu.make_async_copy(wid_hbm, wid_ref, small.at[1]),
    ]

    def start(s, _):
        block_copy(s).start()
        return 0

    lax.fori_loop(0, NSAMP, start, 0)
    for copy in copies:
        copy.start()

    filt = filt_ref[...].astype(F32)
    for j in range(TAPB):
        for part in range(2):
            f_ref[part, j : j + 1, :] = filt[part : part + 1, j * BLK : (j + 1) * BLK]
    row_of = lax.broadcasted_iota(jnp.int32, (BLK, BLK), 0)
    col_of = lax.broadcasted_iota(jnp.int32, (BLK, BLK), 1)
    exchange = jnp.where(row_of + col_of == BLK - 1, 1.0, 0.0).astype(BF)
    r_ref[...] = jnp.zeros_like(r_ref)
    for part in range(2):
        r_ref[part, 1 : 1 + TAPB, :] = dot(f_ref[part].astype(BF), exchange)

    def table(j):
        o = j * 2 * BLK

        def spread(part):
            row = jnp.concatenate([r_ref[part, j + 1 : j + 2, :], r_ref[part, j : j + 1, :]], axis=1)
            wide = jnp.broadcast_to(row, (BLK, 2 * BLK))
            return pltpu.roll(wide, BLK + 1, 1, stride=1, stride_axis=0)[:, :BLK]

        re = spread(0)
        im = spread(1)
        g_ref[o : o + BLK, 0:BLK] = re.astype(BF)
        g_ref[o : o + BLK, BLK:] = im.astype(BF)
        g_ref[o + BLK : o + 2 * BLK, 0:BLK] = (-im).astype(BF)
        g_ref[o + BLK : o + 2 * BLK, BLK:] = re.astype(BF)

    def finish(s, _):
        block_copy(s).wait()
        return 0

    lane = lax.broadcasted_iota(jnp.int32, (1, BLK), 1)

    def migrate(b):
        row = jnp.where(lane < wid_ref[b], w_ref[b : b + 1, :], 0.0)
        row = jnp.concatenate([row, jnp.zeros_like(row)], axis=1)
        row = pltpu.roll(jnp.broadcast_to(row, (8, 2 * BLK)), off_ref[b], 1)[0:1]
        wide = jnp.broadcast_to(row, (BLK, 2 * BLK))
        band = pltpu.roll(wide, 0, 1, stride=1, stride_axis=0).astype(BF)
        window = jnp.concatenate([c_ref[b], c_ref[b + 1]], axis=1)
        moved = lax.dot_general(band, window, NT, preferred_element_type=F32)
        out_ref[b * BLK : (b + 1) * BLK, :] = moved.astype(BF)

    w_ref[:, 0 : coef_ref.shape[1]] = coef_ref[...].astype(F32)
    for copy in copies:
        copy.wait()
    for j in range(EARLY):
        table(j)
    lax.fori_loop(0, NSAMP, finish, 0)

    done, moved = 0, 0
    for count in GROUPS:
        rows = count * BLK
        acc = jnp.zeros((rows, 2 * BLK), F32)
        for j in range(NOUT):
            r0 = (done + j) * BLK
            both = jnp.concatenate([x_ref[0, r0 : r0 + rows, :], x_ref[1, r0 : r0 + rows, :]], axis=1)
            acc = acc + dot(both, g_ref[j * 2 * BLK : (j + 1) * 2 * BLK, :])
            if done == 0 and j + EARLY < NOUT:
                table(j + EARLY)
            if j % 3 == 2 and moved < done - 1:
                migrate(moved)
                moved += 1
        out = acc.astype(BF)
        for b in range(count):
            part = out[b * BLK : (b + 1) * BLK]
            c_ref[done + b, 0:BLK, :] = part[:, :BLK]
            c_ref[done + b, BLK:, :] = part[:, BLK:]
        done += count
    for b in range(moved, NBLK):
        migrate(b)


def compress(raw, range_filter, offsets, widths, coefs):
    vmem = pl.BlockSpec(memory_space=pltpu.VMEM)
    hbm = pl.BlockSpec(memory_space=pltpu.HBM)
    return pl.pallas_call(
        compress_kernel,
        out_shape=jax.ShapeDtypeStruct((NBLK * BLK, 2 * BLK), BF),
        in_specs=[hbm, hbm, vmem, vmem, hbm],
        out_specs=vmem,
        scratch_shapes=[
            pltpu.VMEM((2, NSAMP * BLK, BLK), BF),
            pltpu.VMEM((NOUT * 2 * BLK, 2 * BLK), BF),
            pltpu.VMEM((NOUT, 2 * BLK, BLK), BF),
            pltpu.VMEM((2, TAPB, BLK), F32),
            pltpu.VMEM((2, TAPB + 8, BLK), F32),
            pltpu.VMEM((NBLK, BLK), F32),
            pltpu.SMEM((NBLK,), jnp.int32),
            pltpu.SMEM((NBLK,), jnp.int32),
            pltpu.SemaphoreType.DMA((NSAMP,)),
            pltpu.SemaphoreType.DMA((2,)),
        ],
        compiler_params=pltpu.CompilerParams(vmem_limit_bytes=VMEM),
        cost_estimate=pl.CostEstimate(flops=18_300_000_000, bytes_accessed=8_000_000, transcendentals=0),
    )(offsets, widths, range_filter, coefs, raw)


def split(table):
    hi = table.astype(np.float32).astype(jnp.bfloat16)
    lo = (table - hi.astype(np.float64)).astype(np.float32).astype(jnp.bfloat16)
    return hi, lo


def angles(rows, cols, period):
    return 2.0 * np.pi * (np.outer(rows, cols) % period) / period


def complex_table(theta, sign):
    c, s = np.cos(theta), sign * np.sin(theta)
    return split(np.block([[c, -s], [s, c]]))


def stacked_table(theta, sign):
    return np.concatenate(complex_table(theta, sign), axis=0)


def left_table(theta, sign):
    hi, lo = complex_table(theta, sign)
    return np.concatenate([hi, hi, lo], axis=1)


def right_table(theta, sign):
    hi, lo = complex_table(theta, sign)
    return np.concatenate([hi.T, hi.T, lo.T], axis=0)


def parts(value):
    hi = value.astype(BF)
    return hi, (value - hi.astype(F32)).astype(BF)


def source_order(n_az, n_rg):
    s = np.arange(n_az * n_rg)
    return (s % n_az) * n_rg + s // n_az


def twiddle():
    theta = angles(np.arange(N1), np.arange(BLK), N1 * BLK)
    return np.stack([np.cos(theta), np.sin(theta)]).astype(np.float32)


def filter_kernel(taps_ref, w1_ref, tw_ref, wp_ref, h_ref):
    def pair(i, _):
        both = jnp.concatenate([taps_ref[2 * i], taps_ref[2 * i + 1]], axis=1)
        first = dot(w1_ref[...], both)
        first = first[: 2 * N1] + first[2 * N1 :]
        for u in range(2):
            re = first[:N1, u * BLK : (u + 1) * BLK]
            im = first[N1:, u * BLK : (u + 1) * BLK]
            c, s = tw_ref[0], tw_ref[1]
            hi, lo = parts(jnp.concatenate([re * c - im * s, im * c + re * s], axis=1))
            second = dot(jnp.concatenate([hi, lo, hi], axis=1), wp_ref[...])
            h_ref[2 * i + u] = second * (1.0 / (N1 * BLK))
        return 0

    lax.fori_loop(0, NBIN // 2, pair, 0)


def filter_spectrum(taps):
    w1 = stacked_table(angles(np.arange(N1), np.arange(MFIL), N1), 1.0)
    wp = right_table(angles(np.arange(BLK), np.arange(BLK), BLK), 1.0)
    vmem = pl.BlockSpec(memory_space=pltpu.VMEM)
    return pl.pallas_call(
        filter_kernel,
        out_shape=jax.ShapeDtypeStruct((NBIN, N1, 2 * BLK), F32),
        in_specs=[vmem] * 4,
        out_specs=vmem,
        compiler_params=pltpu.CompilerParams(vmem_limit_bytes=VMEM),
        cost_estimate=pl.CostEstimate(flops=4_000_000_000, bytes_accessed=8_000_000, transcendentals=0),
    )(taps, jnp.asarray(w1), jnp.asarray(twiddle()), jnp.asarray(wp))


def focus_kernel(x_hbm, h_hbm, w1_hbm, tw_hbm, wp_hbm, wq_hbm, w3_hbm, out_hbm, *scratch):
    x_ref, h_ref, w1_ref, tw_ref, wp_ref, wq_ref, w3_ref, out_ref, s_ref, z_ref = scratch[:10]
    stage1, stage2, stage3 = scratch[10:12], scratch[12:14], scratch[14:16]
    x_sems, t_sems, o_sems = scratch[16:]
    piece = MSRC // PIECES
    arriving = []
    for i in range(PIECES):
        part = pl.ds(i * piece, piece)
        arriving.append(pltpu.make_async_copy(x_hbm.at[part], x_ref.at[part], x_sems.at[i]))
    tables = [(w1_hbm, w1_ref), (tw_hbm, tw_ref), (h_hbm, h_ref), (wp_hbm, wp_ref), (wq_hbm, wq_ref), (w3_hbm, w3_ref)]
    tables = [pltpu.make_async_copy(src, dst, t_sems.at[i]) for i, (src, dst) in enumerate(tables)]
    for copy in arriving + tables:
        copy.start()

    def widen(m, _):
        part = x_ref[m].astype(F32)
        s_ref[pl.ds(pl.multiple_of(m * PITCH, 8), NBIN), :] = part[:, :BLK]
        s_ref[pl.ds(pl.multiple_of((MSRC + m) * PITCH, 8), NBIN), :] = part[:, BLK:]
        return 0

    for i in range(PIECES):
        arriving[i].wait()
        lax.fori_loop(i * piece, (i + 1) * piece, widen, 0, unroll=8)
    for copy in tables:
        copy.wait()

    def load(b):
        return s_ref[pl.ds(b, 2 * MSRC, stride=PITCH), :].astype(BF)

    def coarse(i, to):
        both = jnp.concatenate([load(SIDE * i + u) for u in range(SIDE)], axis=1)
        first = dot(w1_ref[...], both)
        first = first[: 2 * N1] + first[2 * N1 :]
        c, s = tw_ref[0], tw_ref[1]
        for u in range(SIDE):
            rows = slice(u * N1, (u + 1) * N1)
            re = first[:N1, u * BLK : (u + 1) * BLK]
            im = first[N1:, u * BLK : (u + 1) * BLK]
            to[rows, 0:BLK] = (re * c + im * s).astype(BF)
            to[rows, BLK:] = (im * c - re * s).astype(BF)

    def wide(at):
        return jnp.concatenate([at[...], at[:, : 2 * BLK]], axis=1)

    def fine(i, at, to):
        spectrum = dot(jnp.concatenate([at[...], at[...]], axis=1), wp_ref[...])
        for u in range(SIDE):
            rows = slice(u * N1, (u + 1) * N1)
            xr = spectrum[rows, :BLK]
            xi = spectrum[rows, BLK:]
            hr = h_ref[SIDE * i + u, :, :BLK]
            hi = h_ref[SIDE * i + u, :, BLK:]
            to[rows, 0:BLK], to[rows, 2 * BLK : 3 * BLK] = parts(xr * hr - xi * hi)
            to[rows, BLK : 2 * BLK], to[rows, 3 * BLK :] = parts(xr * hi + xi * hr)

    def fine_back(at, to):
        back = dot(wide(at), wq_ref[...])
        c, s = tw_ref[0], tw_ref[1]
        for u in range(SIDE):
            lanes = slice(u * BLK, (u + 1) * BLK)
            re = back[u * N1 : (u + 1) * N1, :BLK]
            im = back[u * N1 : (u + 1) * N1, BLK:]
            to[0:N1, lanes], to[2 * N1 : 3 * N1, lanes] = parts(re * c - im * s)
            to[N1 : 2 * N1, lanes], to[3 * N1 :, lanes] = parts(im * c + re * s)

    def coarse_back(i, at):
        last = dot(w3_ref[...], jnp.concatenate([at[...], at[: 2 * N1, :]], axis=0))
        for u in range(SIDE):
            z_ref[pl.ds(SIDE * i + u, 2 * MOUT, stride=PITCH), :] = last[:, u * BLK : (u + 1) * BLK]

    pairs = NBIN // SIDE

    def step(q, parity, first, last):
        if first <= 3 <= last:
            coarse_back(q - 3, stage3[1 - parity])
        if first <= 2 <= last:
            fine_back(stage2[parity], stage3[parity])
        if first <= 1 <= last:
            fine(q - 1, stage1[1 - parity], stage2[1 - parity])
        if first <= 0 <= last:
            coarse(q, stage1[parity])

    for q in range(3):
        step(q, q % 2, 0, q)

    def two(i, _):
        step(3 + 2 * i, 1, 0, 3)
        step(4 + 2 * i, 0, 0, 3)
        return 0

    lax.fori_loop(0, (pairs - 4) // 2, two, 0)
    step(pairs - 1, (pairs - 1) % 2, 0, 3)
    for q in range(pairs, pairs + 3):
        step(q, q % 2, q - pairs + 1, 3)

    n_az = out_ref.shape[0]
    blocks = MOUT // n_az

    def leave(a):
        return pltpu.make_async_copy(out_ref.at[a], out_hbm.at[a], o_sems.at[a])

    def narrow(a, _):
        for part in range(2):
            for m in range(blocks):
                o = pl.multiple_of(((part * n_az + a) * blocks + m) * PITCH, 8)
                row = (part * blocks + m) * NBIN
                out_ref[a, row : row + NBIN, :] = z_ref[pl.ds(o, NBIN), :].astype(BF)
        leave(a).start()
        return 0

    lax.fori_loop(0, n_az, narrow, 0)

    def left(a, _):
        leave(a).wait()
        return 0

    lax.fori_loop(0, n_az, left, 0)


def focus(x, spectrum, n_az, n_rg):
    order = source_order(n_az, n_rg)
    w1 = stacked_table(angles(np.arange(N1), order, N1), -1.0)
    hi, lo = complex_table(angles(np.arange(BLK), np.arange(BLK), BLK), -1.0)
    wp = np.concatenate([hi.T, lo.T], axis=0)
    wq = right_table(angles(np.arange(BLK), np.arange(BLK), BLK), 1.0)
    w3 = left_table(angles(np.arange(MOUT), np.arange(N1), N1), 1.0)
    hbm = pl.BlockSpec(memory_space=pltpu.HBM)
    out = (n_az, 2 * MOUT // n_az * NBIN, BLK)
    tables = [(w1, BF), (twiddle(), F32), (wp, BF), (wq, BF), (w3, BF)]
    return pl.pallas_call(
        focus_kernel,
        out_shape=jax.ShapeDtypeStruct(out, BF),
        in_specs=[hbm] * 7,
        out_specs=hbm,
        scratch_shapes=[
            pltpu.VMEM(x.shape, BF),
            pltpu.VMEM(spectrum.shape, F32),
            *[pltpu.VMEM(table.shape, kind) for table, kind in tables],
            pltpu.VMEM(out, BF),
            pltpu.VMEM((2 * MSRC * PITCH, BLK), F32),
            pltpu.VMEM((2 * MOUT * PITCH, BLK), F32),
            *[pltpu.VMEM((SIDE * N1, 2 * BLK), BF)] * 2,
            *[pltpu.VMEM((SIDE * N1, 4 * BLK), BF)] * 2,
            *[pltpu.VMEM((4 * N1, SIDE * BLK), BF)] * 2,
            pltpu.SemaphoreType.DMA((PIECES,)),
            pltpu.SemaphoreType.DMA((6,)),
            pltpu.SemaphoreType.DMA((n_az,)),
        ],
        compiler_params=pltpu.CompilerParams(vmem_limit_bytes=VMEM),
        cost_estimate=pl.CostEstimate(flops=6_000_000_000, bytes_accessed=10_000_000, transcendentals=0),
    )(x, spectrum, *[jnp.asarray(table) for table, _ in tables])


def turn_kernel(y_hbm, out_hbm, y_ref, out_ref, in_sems, out_sems):
    n_az, rows, _ = y_ref.shape
    piece = rows // TURNS
    arriving = []
    for i in range(TURNS):
        part = pl.ds(i * piece, piece)
        arriving.append(pltpu.make_async_copy(y_hbm.at[:, part, :], y_ref.at[:, part, :], in_sems.at[i]))
        arriving[-1].start()
    row_of = lax.broadcasted_iota(jnp.int32, (BLK, BLK), 0)
    col_of = lax.broadcasted_iota(jnp.int32, (BLK, BLK), 1)
    unit = jnp.where(row_of == col_of, 1.0, 0.0).astype(BF)
    leaving = []
    for i in range(TURNS):
        arriving[i].wait()
        for k in range(i * piece // NBIN, (i + 1) * piece // NBIN):
            part = y_ref[:, k * NBIN : (k + 1) * NBIN, :].reshape(n_az * NBIN, BLK)
            out_ref[k * BLK : (k + 1) * BLK, :] = lax.dot_general(unit, part, NT, preferred_element_type=F32)
        done = pl.ds(i * piece // NBIN * BLK, piece // NBIN * BLK)
        leaving.append(pltpu.make_async_copy(out_ref.at[done, :], out_hbm.at[done, :], out_sems.at[i]))
        leaving[-1].start()
    for copy in leaving:
        copy.wait()


def turn(y):
    n_az, rows, _ = y.shape
    out = (rows // NBIN * BLK, n_az * NBIN)
    hbm = pl.BlockSpec(memory_space=pltpu.HBM)
    image = pl.pallas_call(
        turn_kernel,
        out_shape=jax.ShapeDtypeStruct(out, F32),
        in_specs=[hbm],
        out_specs=hbm,
        scratch_shapes=[
            pltpu.VMEM(y.shape, BF),
            pltpu.VMEM(out, F32),
            pltpu.SemaphoreType.DMA((TURNS,)),
            pltpu.SemaphoreType.DMA((TURNS,)),
        ],
        compiler_params=pltpu.CompilerParams(vmem_limit_bytes=VMEM),
        cost_estimate=pl.CostEstimate(flops=0, bytes_accessed=6_000_000, transcendentals=0),
    )(y)
    return image.reshape(2, out[0] // 2, out[1])


def own_taps(az_filter, az_lengths):
    first = lax.axis_index("az") * NBIN
    taps = lax.dynamic_slice_in_dim(az_filter, first, NBIN, 2)
    lengths = lax.dynamic_slice_in_dim(az_lengths, first, NBIN, 0)
    kept = jnp.arange(taps.shape[1])[:, None] < lengths[None, :]
    taps = jnp.where(kept[None], taps, jnp.zeros((), BF))
    return taps.transpose(2, 0, 1).reshape(NBIN, 2 * MFIL, BLK)


def per_device(raw, range_filter, mig_offsets, mig_widths, mig_coefs, az_filter, az_lengths):
    n_az, n_rg = lax.axis_size("az"), lax.axis_size("rg")
    moved = compress(raw, range_filter, mig_offsets, mig_widths, mig_coefs)
    moved = moved.reshape(n_rg * n_az, NBIN, 2 * BLK)
    x = lax.all_to_all(moved, ("rg", "az"), 0, 0, tiled=True)
    spectrum = filter_spectrum(own_taps(az_filter, az_lengths))
    y = focus(x, spectrum, n_az, n_rg)
    y = lax.all_to_all(y, "az", 0, 0, tiled=True)
    return turn(y)


def solution(mesh):
    return jax.shard_map(
        per_device,
        mesh=mesh,
        in_specs=(P(None, ("az", "rg"), None), P(), P(), P(), P(), P(None, None, "rg"), P("rg")),
        out_specs=P(None, "az", "rg"),
        check_vma=False,
    )
```

```python
import functools
import math

import jax
import jax.numpy as jnp
import numpy as np
from jax import lax
from jax.experimental import pallas as pl
from jax.experimental.pallas import tpu as pltpu
from jax.sharding import PartitionSpec as P

BF = jnp.bfloat16
F32 = jnp.float32
BLK = 128
TAPB = 32
NBLK = 32
NOUT = 33
NSAMP = 65
N1 = 160
MSRC = 128
MOUT = 128
MFIL = 32
NBIN = 32
PIECES = 8
TURNS = 4
SIDE = 8
PITCH = 40
VMEM = 60 * 1024 * 1024
GROUPS = (11, 11, 11)
EARLY = 8
NT = (((1,), (1,)), ((), ()))


def dot(a, b):
    return jnp.dot(a, b, preferred_element_type=F32)


def compress_kernel(
    off_hbm, wid_hbm, filt_ref, coef_ref, raw_hbm, out_hbm, out_ref, x_ref, g_ref, c_ref, f_ref, r_ref, w_ref, off_ref, wid_ref, sems, small, outs
):
    def block_copy(s):
        o = pl.multiple_of(s * BLK, BLK)
        return pltpu.make_async_copy(raw_hbm.at[:, :, pl.ds(o, BLK)], x_ref.at[:, pl.ds(o, BLK), :], sems.at[s])

    copies = [
        pltpu.make_async_copy(off_hbm, off_ref, small.at[0]),
        pltpu.make_async_copy(wid_hbm, wid_ref, small.at[1]),
    ]

    def start(s, _):
        block_copy(s).start()
        return 0

    lax.fori_loop(0, NSAMP, start, 0)
    for copy in copies:
        copy.start()

    filt = filt_ref[...].astype(F32)
    for j in range(TAPB):
        for part in range(2):
            f_ref[part, j : j + 1, :] = filt[part : part + 1, j * BLK : (j + 1) * BLK]
    row_of = lax.broadcasted_iota(jnp.int32, (BLK, BLK), 0)
    col_of = lax.broadcasted_iota(jnp.int32, (BLK, BLK), 1)
    exchange = jnp.where(row_of + col_of == BLK - 1, 1.0, 0.0).astype(BF)
    r_ref[...] = jnp.zeros_like(r_ref)
    for part in range(2):
        r_ref[part, 1 : 1 + TAPB, :] = dot(f_ref[part].astype(BF), exchange)

    def table(j):
        o = j * 2 * BLK

        def spread(part):
            row = jnp.concatenate([r_ref[part, j + 1 : j + 2, :], r_ref[part, j : j + 1, :]], axis=1)
            wide = jnp.broadcast_to(row, (BLK, 2 * BLK))
            return pltpu.roll(wide, BLK + 1, 1, stride=1, stride_axis=0)[:, :BLK]

        re = spread(0)
        im = spread(1)
        g_ref[o : o + BLK, 0:BLK] = re.astype(BF)
        g_ref[o : o + BLK, BLK:] = im.astype(BF)
        g_ref[o + BLK : o + 2 * BLK, 0:BLK] = (-im).astype(BF)
        g_ref[o + BLK : o + 2 * BLK, BLK:] = re.astype(BF)

    def finish(s, _):
        block_copy(s).wait()
        return 0

    lane = lax.broadcasted_iota(jnp.int32, (1, BLK), 1)

    def migrate(b):
        row = jnp.where(lane < wid_ref[b], w_ref[b : b + 1, :], 0.0)
        row = jnp.concatenate([row, jnp.zeros_like(row)], axis=1)
        row = pltpu.roll(jnp.broadcast_to(row, (8, 2 * BLK)), off_ref[b], 1)[0:1]
        wide = jnp.broadcast_to(row, (BLK, 2 * BLK))
        band = pltpu.roll(wide, 0, 1, stride=1, stride_axis=0).astype(BF)
        window = jnp.concatenate([c_ref[b], c_ref[b + 1]], axis=1)
        moved = lax.dot_general(band, window, NT, preferred_element_type=F32)
        out_ref[b * BLK : (b + 1) * BLK, :] = moved.astype(BF)

    w_ref[:, 0 : coef_ref.shape[1]] = coef_ref[...].astype(F32)
    for copy in copies:
        copy.wait()
    for j in range(EARLY):
        table(j)
    lax.fori_loop(0, NSAMP, finish, 0)

    done, moved = 0, 0
    for count in GROUPS:
        rows = count * BLK
        acc = jnp.zeros((rows, 2 * BLK), F32)
        for j in range(NOUT):
            r0 = (done + j) * BLK
            both = jnp.concatenate([x_ref[0, r0 : r0 + rows, :], x_ref[1, r0 : r0 + rows, :]], axis=1)
            acc = acc + dot(both, g_ref[j * 2 * BLK : (j + 1) * 2 * BLK, :])
            if done == 0 and j + EARLY < NOUT:
                table(j + EARLY)
            if j % 3 == 2 and moved < done - 1:
                migrate(moved)
                moved += 1
        out = acc.astype(BF)
        for b in range(count):
            part = out[b * BLK : (b + 1) * BLK]
            c_ref[done + b, 0:BLK, :] = part[:, :BLK]
            c_ref[done + b, BLK:, :] = part[:, BLK:]
        done += count
    early = pl.ds(0, moved * BLK)
    late = pl.ds(moved * BLK, (NBLK - moved) * BLK)
    sending = [pltpu.make_async_copy(out_ref.at[part, :], out_hbm.at[part, :], outs.at[i]) for i, part in enumerate((early, late))]
    sending[0].start()
    for b in range(moved, NBLK):
        migrate(b)
    sending[1].start()
    for copy in sending:
        copy.wait()


def compress(raw, range_filter, offsets, widths, coefs):
    vmem = pl.BlockSpec(memory_space=pltpu.VMEM)
    hbm = pl.BlockSpec(memory_space=pltpu.HBM)
    return pl.pallas_call(
        compress_kernel,
        out_shape=jax.ShapeDtypeStruct((NBLK * BLK, 2 * BLK), BF),
        in_specs=[hbm, hbm, vmem, vmem, hbm],
        out_specs=pl.BlockSpec(memory_space=pltpu.HBM),
        scratch_shapes=[
            pltpu.VMEM((NBLK * BLK, 2 * BLK), BF),
            pltpu.VMEM((2, NSAMP * BLK, BLK), BF),
            pltpu.VMEM((NOUT * 2 * BLK, 2 * BLK), BF),
            pltpu.VMEM((NOUT, 2 * BLK, BLK), BF),
            pltpu.VMEM((2, TAPB, BLK), F32),
            pltpu.VMEM((2, TAPB + 8, BLK), F32),
            pltpu.VMEM((NBLK, BLK), F32),
            pltpu.SMEM((NBLK,), jnp.int32),
            pltpu.SMEM((NBLK,), jnp.int32),
            pltpu.SemaphoreType.DMA((NSAMP,)),
            pltpu.SemaphoreType.DMA((2,)),
            pltpu.SemaphoreType.DMA((2,)),
        ],
        compiler_params=pltpu.CompilerParams(vmem_limit_bytes=VMEM),
        cost_estimate=pl.CostEstimate(flops=18_300_000_000, bytes_accessed=8_000_000, transcendentals=0),
    )(offsets, widths, range_filter, coefs, raw)


def split(table):
    hi = table.astype(np.float32).astype(jnp.bfloat16)
    lo = (table - hi.astype(np.float64)).astype(np.float32).astype(jnp.bfloat16)
    return hi, lo


def angles(rows, cols, period):
    return 2.0 * np.pi * (np.outer(rows, cols) % period) / period


def complex_table(theta, sign):
    c, s = np.cos(theta), sign * np.sin(theta)
    return split(np.block([[c, -s], [s, c]]))


def stacked_table(theta, sign):
    return np.concatenate(complex_table(theta, sign), axis=0)


def left_table(theta, sign):
    hi, lo = complex_table(theta, sign)
    return np.concatenate([hi, hi, lo], axis=1)


def right_table(theta, sign):
    hi, lo = complex_table(theta, sign)
    return np.concatenate([hi.T, hi.T, lo.T], axis=0)


def parts(value):
    hi = value.astype(BF)
    return hi, (value - hi.astype(F32)).astype(BF)


def source_order(n_az, n_rg):
    s = np.arange(n_az * n_rg)
    return (s % n_az) * n_rg + s // n_az


def twiddle():
    theta = angles(np.arange(N1), np.arange(BLK), N1 * BLK)
    return np.stack([np.cos(theta), np.sin(theta)]).astype(np.float32)


def filter_kernel(taps_ref, w1_ref, tw_ref, wp_ref, h_ref):
    def pair(i, _):
        both = jnp.concatenate([taps_ref[2 * i], taps_ref[2 * i + 1]], axis=1)
        first = dot(w1_ref[...], both)
        first = first[: 2 * N1] + first[2 * N1 :]
        for u in range(2):
            re = first[:N1, u * BLK : (u + 1) * BLK]
            im = first[N1:, u * BLK : (u + 1) * BLK]
            c, s = tw_ref[0], tw_ref[1]
            hi, lo = parts(jnp.concatenate([re * c - im * s, im * c + re * s], axis=1))
            second = dot(jnp.concatenate([hi, lo, hi], axis=1), wp_ref[...])
            h_ref[2 * i + u] = second * (1.0 / (N1 * BLK))
        return 0

    lax.fori_loop(0, NBIN // 2, pair, 0)


def filter_spectrum(taps):
    w1 = stacked_table(angles(np.arange(N1), np.arange(MFIL), N1), 1.0)
    wp = right_table(angles(np.arange(BLK), np.arange(BLK), BLK), 1.0)
    vmem = pl.BlockSpec(memory_space=pltpu.VMEM)
    return pl.pallas_call(
        filter_kernel,
        out_shape=jax.ShapeDtypeStruct((NBIN, N1, 2 * BLK), F32),
        in_specs=[vmem] * 4,
        out_specs=vmem,
        compiler_params=pltpu.CompilerParams(vmem_limit_bytes=VMEM),
        cost_estimate=pl.CostEstimate(flops=4_000_000_000, bytes_accessed=8_000_000, transcendentals=0),
    )(taps, jnp.asarray(w1), jnp.asarray(twiddle()), jnp.asarray(wp))


def focus_kernel(x_hbm, h_hbm, w1_hbm, tw_hbm, wp_hbm, wq_hbm, w3_hbm, out_hbm, *scratch):
    x_ref, h_ref, w1_ref, tw_ref, wp_ref, wq_ref, w3_ref, out_ref, s_ref, z_ref = scratch[:10]
    stage1, stage2, stage3 = scratch[10:12], scratch[12:14], scratch[14:16]
    x_sems, t_sems, o_sems = scratch[16:]
    piece = MSRC // PIECES
    arriving = []
    for i in range(PIECES):
        part = pl.ds(i * piece, piece)
        arriving.append(pltpu.make_async_copy(x_hbm.at[part], x_ref.at[part], x_sems.at[i]))
    tables = [(w1_hbm, w1_ref), (tw_hbm, tw_ref), (h_hbm, h_ref), (wp_hbm, wp_ref), (wq_hbm, wq_ref), (w3_hbm, w3_ref)]
    tables = [pltpu.make_async_copy(src, dst, t_sems.at[i]) for i, (src, dst) in enumerate(tables)]
    for copy in arriving + tables:
        copy.start()

    def widen(m, _):
        part = x_ref[m].astype(F32)
        s_ref[pl.ds(pl.multiple_of(m * PITCH, 8), NBIN), :] = part[:, :BLK]
        s_ref[pl.ds(pl.multiple_of((MSRC + m) * PITCH, 8), NBIN), :] = part[:, BLK:]
        return 0

    for i in range(PIECES):
        arriving[i].wait()
        lax.fori_loop(i * piece, (i + 1) * piece, widen, 0, unroll=8)
    for copy in tables:
        copy.wait()

    def load(b):
        return s_ref[pl.ds(b, 2 * MSRC, stride=PITCH), :].astype(BF)

    def coarse(i, to):
        both = jnp.concatenate([load(SIDE * i + u) for u in range(SIDE)], axis=1)
        first = dot(w1_ref[...], both)
        first = first[: 2 * N1] + first[2 * N1 :]
        c, s = tw_ref[0], tw_ref[1]
        for u in range(SIDE):
            rows = slice(u * N1, (u + 1) * N1)
            re = first[:N1, u * BLK : (u + 1) * BLK]
            im = first[N1:, u * BLK : (u + 1) * BLK]
            to[rows, 0:BLK] = (re * c + im * s).astype(BF)
            to[rows, BLK:] = (im * c - re * s).astype(BF)

    def wide(at):
        return jnp.concatenate([at[...], at[:, : 2 * BLK]], axis=1)

    def fine(i, at, to):
        spectrum = dot(jnp.concatenate([at[...], at[...]], axis=1), wp_ref[...])
        for u in range(SIDE):
            rows = slice(u * N1, (u + 1) * N1)
            xr = spectrum[rows, :BLK]
            xi = spectrum[rows, BLK:]
            hr = h_ref[SIDE * i + u, :, :BLK]
            hi = h_ref[SIDE * i + u, :, BLK:]
            to[rows, 0:BLK], to[rows, 2 * BLK : 3 * BLK] = parts(xr * hr - xi * hi)
            to[rows, BLK : 2 * BLK], to[rows, 3 * BLK :] = parts(xr * hi + xi * hr)

    def fine_back(at, to):
        back = dot(wide(at), wq_ref[...])
        c, s = tw_ref[0], tw_ref[1]
        for u in range(SIDE):
            lanes = slice(u * BLK, (u + 1) * BLK)
            re = back[u * N1 : (u + 1) * N1, :BLK]
            im = back[u * N1 : (u + 1) * N1, BLK:]
            to[0:N1, lanes], to[2 * N1 : 3 * N1, lanes] = parts(re * c - im * s)
            to[N1 : 2 * N1, lanes], to[3 * N1 :, lanes] = parts(im * c + re * s)

    def coarse_back(i, at):
        last = dot(w3_ref[...], jnp.concatenate([at[...], at[: 2 * N1, :]], axis=0))
        for u in range(SIDE):
            z_ref[pl.ds(SIDE * i + u, 2 * MOUT, stride=PITCH), :] = last[:, u * BLK : (u + 1) * BLK]

    pairs = NBIN // SIDE

    def step(q, parity, first, last):
        if first <= 3 <= last:
            coarse_back(q - 3, stage3[1 - parity])
        if first <= 2 <= last:
            fine_back(stage2[parity], stage3[parity])
        if first <= 1 <= last:
            fine(q - 1, stage1[1 - parity], stage2[1 - parity])
        if first <= 0 <= last:
            coarse(q, stage1[parity])

    for q in range(3):
        step(q, q % 2, 0, q)

    def two(i, _):
        step(3 + 2 * i, 1, 0, 3)
        step(4 + 2 * i, 0, 0, 3)
        return 0

    lax.fori_loop(0, (pairs - 4) // 2, two, 0)
    step(pairs - 1, (pairs - 1) % 2, 0, 3)
    for q in range(pairs, pairs + 3):
        step(q, q % 2, q - pairs + 1, 3)

    n_az = out_ref.shape[0]
    blocks = MOUT // n_az

    def leave(a):
        return pltpu.make_async_copy(out_ref.at[a], out_hbm.at[a], o_sems.at[a])

    def narrow(a, _):
        for part in range(2):
            for m in range(blocks):
                o = pl.multiple_of(((part * n_az + a) * blocks + m) * PITCH, 8)
                row = (part * blocks + m) * NBIN
                out_ref[a, row : row + NBIN, :] = z_ref[pl.ds(o, NBIN), :].astype(BF)
        leave(a).start()
        return 0

    lax.fori_loop(0, n_az, narrow, 0)

    def left(a, _):
        leave(a).wait()
        return 0

    lax.fori_loop(0, n_az, left, 0)


def focus(x, spectrum, n_az, n_rg):
    order = source_order(n_az, n_rg)
    w1 = stacked_table(angles(np.arange(N1), order, N1), -1.0)
    hi, lo = complex_table(angles(np.arange(BLK), np.arange(BLK), BLK), -1.0)
    wp = np.concatenate([hi.T, lo.T], axis=0)
    wq = right_table(angles(np.arange(BLK), np.arange(BLK), BLK), 1.0)
    w3 = left_table(angles(np.arange(MOUT), np.arange(N1), N1), 1.0)
    hbm = pl.BlockSpec(memory_space=pltpu.HBM)
    out = (n_az, 2 * MOUT // n_az * NBIN, BLK)
    tables = [(w1, BF), (twiddle(), F32), (wp, BF), (wq, BF), (w3, BF)]
    return pl.pallas_call(
        focus_kernel,
        out_shape=jax.ShapeDtypeStruct(out, BF),
        in_specs=[hbm] * 7,
        out_specs=hbm,
        scratch_shapes=[
            pltpu.VMEM(x.shape, BF),
            pltpu.VMEM(spectrum.shape, F32),
            *[pltpu.VMEM(table.shape, kind) for table, kind in tables],
            pltpu.VMEM(out, BF),
            pltpu.VMEM((2 * MSRC * PITCH, BLK), F32),
            pltpu.VMEM((2 * MOUT * PITCH, BLK), F32),
            *[pltpu.VMEM((SIDE * N1, 2 * BLK), BF)] * 2,
            *[pltpu.VMEM((SIDE * N1, 4 * BLK), BF)] * 2,
            *[pltpu.VMEM((4 * N1, SIDE * BLK), BF)] * 2,
            pltpu.SemaphoreType.DMA((PIECES,)),
            pltpu.SemaphoreType.DMA((6,)),
            pltpu.SemaphoreType.DMA((n_az,)),
        ],
        compiler_params=pltpu.CompilerParams(vmem_limit_bytes=VMEM),
        cost_estimate=pl.CostEstimate(flops=6_000_000_000, bytes_accessed=10_000_000, transcendentals=0),
    )(x, spectrum, *[jnp.asarray(table) for table, _ in tables])


def turn_kernel(y_hbm, out_hbm, y_ref, out_ref, in_sems, out_sems):
    n_az, rows, _ = y_ref.shape
    piece = rows // TURNS
    arriving = []
    for i in range(TURNS):
        part = pl.ds(i * piece, piece)
        arriving.append(pltpu.make_async_copy(y_hbm.at[:, part, :], y_ref.at[:, part, :], in_sems.at[i]))
        arriving[-1].start()
    row_of = lax.broadcasted_iota(jnp.int32, (BLK, BLK), 0)
    col_of = lax.broadcasted_iota(jnp.int32, (BLK, BLK), 1)
    unit = jnp.where(row_of == col_of, 1.0, 0.0).astype(BF)
    leaving = []
    for i in range(TURNS):
        arriving[i].wait()
        for k in range(i * piece // NBIN, (i + 1) * piece // NBIN):
            part = y_ref[:, k * NBIN : (k + 1) * NBIN, :].reshape(n_az * NBIN, BLK)
            out_ref[k * BLK : (k + 1) * BLK, :] = lax.dot_general(unit, part, NT, preferred_element_type=F32)
        done = pl.ds(i * piece // NBIN * BLK, piece // NBIN * BLK)
        leaving.append(pltpu.make_async_copy(out_ref.at[done, :], out_hbm.at[done, :], out_sems.at[i]))
        leaving[-1].start()
    for copy in leaving:
        copy.wait()


def turn(y):
    n_az, rows, _ = y.shape
    out = (rows // NBIN * BLK, n_az * NBIN)
    hbm = pl.BlockSpec(memory_space=pltpu.HBM)
    image = pl.pallas_call(
        turn_kernel,
        out_shape=jax.ShapeDtypeStruct(out, F32),
        in_specs=[hbm],
        out_specs=hbm,
        scratch_shapes=[
            pltpu.VMEM(y.shape, BF),
            pltpu.VMEM(out, F32),
            pltpu.SemaphoreType.DMA((TURNS,)),
            pltpu.SemaphoreType.DMA((TURNS,)),
        ],
        compiler_params=pltpu.CompilerParams(vmem_limit_bytes=VMEM),
        cost_estimate=pl.CostEstimate(flops=0, bytes_accessed=6_000_000, transcendentals=0),
    )(y)
    return image.reshape(2, out[0] // 2, out[1])


def own_taps(az_filter, az_lengths):
    first = lax.axis_index("az") * NBIN
    taps = lax.dynamic_slice_in_dim(az_filter, first, NBIN, 2)
    lengths = lax.dynamic_slice_in_dim(az_lengths, first, NBIN, 0)
    kept = jnp.arange(taps.shape[1])[:, None] < lengths[None, :]
    taps = jnp.where(kept[None], taps, jnp.zeros((), BF))
    return taps.transpose(2, 0, 1).reshape(NBIN, 2 * MFIL, BLK)


def per_device(raw, range_filter, mig_offsets, mig_widths, mig_coefs, az_filter, az_lengths):
    n_az, n_rg = lax.axis_size("az"), lax.axis_size("rg")
    moved = compress(raw, range_filter, mig_offsets, mig_widths, mig_coefs)
    moved = moved.reshape(n_rg * n_az, NBIN, 2 * BLK)
    x = lax.all_to_all(moved, ("rg", "az"), 0, 0, tiled=True)
    spectrum = filter_spectrum(own_taps(az_filter, az_lengths))
    y = focus(x, spectrum, n_az, n_rg)
    y = lax.all_to_all(y, "az", 0, 0, tiled=True)
    return turn(y)


def solution(mesh):
    return jax.shard_map(
        per_device,
        mesh=mesh,
        in_specs=(P(None, ("az", "rg"), None), P(), P(), P(), P(), P(None, None, "rg"), P("rg")),
        out_specs=P(None, "az", "rg"),
        check_vma=False,
    )
```
